128 devices in a mesh: slab: 64 (over z, x, y), sub: 2 (over core).
Axes of the slice: x: 4, y: 4, z: 4, core: 2. Of those that a mesh axis runs over, the one named last changes fastest.
Arguments:
- right_side: float32 [1024, 8, 128], P('slab'), may hold values from -7.2 to 7.2
- diagonal: float32 [1024, 128], P('slab'), may hold values from 0.02 to 2
- dense_blocks: float32 [1024, 128, 128], P(('slab', 'sub')), may hold values from -0.01171875 to 0.01171875
- tiles: float32 [1024, 8, 128, 128], P('slab', 'sub'), may hold values from -0.005859375 to 0.005859375
- tile_cols: int32 [1024, 8], P('slab', 'sub'), may hold values from 1 to 1023, as said below
- tile_counts: int32 [1024], P('slab'), may hold values from 0 to 8, as said below
Outputs:
- solution_field: float32 [1024, 8, 128], P('slab')
- residual: float32 [1024, 8, 128], P('slab')
The draws below stay inside these ranges and needn't reach their ends.
Inputs may be any that keep to these rules, and one draw needn't show every extreme that they name: `tile_cols`: every slot of block row r below 1023 holds a column c with r < c <= min(r + 16, 1023); in the last block row c = r; the first block row holds column 1. Slots k < tile_counts[r] are live; the first block row has all of them live, the last none.
All inputs are finite; a program needn't handle non-finite values.
Results may differ from the reference program's by a relative error of at most 0.0003.
Values sent between devices are 32-bit elements; how exact they have to be, the bound alone decides.
A program may use at most 64 MiB of HBM per device.

```python
import math
import jax
import jax.numpy as jnp
from jax import lax

BLK = 128
BLK_DEV = 16
TILES_ROW = 8
NRHS = 8
ITERS = 4
NBLK = 1024


def draw_right_side(key, part):
    rows = jnp.arange(NBLK, dtype=jnp.float32)[:, None, None] / (NBLK - 1)
    rising = 0.6 * (1.0 + 2.0 * rows)
    values = jnp.clip(jax.random.normal(key, (NBLK, NRHS, BLK), jnp.float32), -4.0, 4.0)
    return values * rising


def draw_tile_cols(key, part):
    rows = jnp.arange(NBLK, dtype=jnp.int32)[:, None]
    pick = jax.random.randint(key, (NBLK, TILES_ROW), 0, BLK_DEV, dtype=jnp.int32)
    reach = jnp.maximum(jnp.minimum(BLK_DEV, NBLK - 1 - rows), 1)
    offset = 1 + pick % reach
    slot = jnp.arange(TILES_ROW, dtype=jnp.int32)[None, :]
    offset = jnp.where((slot == 0) & (rows % BLK_DEV == 0), reach, offset)
    offset = jnp.where((slot == 1) & (rows % BLK_DEV == 0), 1, offset)
    return jnp.minimum(rows + offset, NBLK - 1).astype(jnp.int32)


def draw_tile_counts(key, part):
    counts = jax.random.randint(key, (NBLK,), 1, TILES_ROW + 1, dtype=jnp.int32)
    rows = jnp.arange(NBLK, dtype=jnp.int32)
    counts = jnp.where(rows == 0, TILES_ROW, counts)
    return jnp.where(rows == NBLK - 1, 0, counts).astype(jnp.int32)


def shard_levels(rng, dims, shards, smallest, largest):
    def one(axis_at, blocks):
        draws = jax.random.uniform(jax.random.fold_in(jax.random.fold_in(rng, 6), axis_at), (blocks,), jnp.float32, smallest / len(shards), largest / len(shards))
        return jnp.repeat(jnp.exp(draws), dims[axis_at] // blocks).reshape((-1,) + (1,) * (len(dims) - axis_at - 1))

    gain = one(*shards[0])
    for cut in shards[1:]:
        gain = gain * one(*cut)
    return gain


def centred(own_key, dims, deviation, most, shards=(), kind=jnp.bfloat16):
    array = deviation * jax.random.normal(own_key, dims, jnp.float32)
    if shards:
        array = array * shard_levels(own_key, dims, shards, -0.22, 0.18)
    return jnp.clip(array, -most, most).astype(kind)


def setup_inputs(seed: int = 0) -> dict:
    keys = jax.random.split(jax.random.key(seed), 7)
    return {
        "right_side": draw_right_side(jax.random.fold_in(keys[6], 71), 0),
        "diagonal": jnp.clip(jnp.exp(math.log(2.0) - 4.6051702 * jax.random.uniform(keys[1], (NBLK, BLK), jnp.float32) ** shard_levels(keys[1], (NBLK, BLK), ((0, 64),), -0.2, 0.2)), 0.02, 2.0),
        "dense_blocks": centred(keys[2], (NBLK, BLK, BLK), (16 * BLK * BLK) ** -0.5, 0.01171875, ((0, 128),), jnp.float32),
        "tiles": centred(keys[3], (NBLK, TILES_ROW, BLK, BLK), (BLK * BLK * TILES_ROW * TILES_ROW) ** -0.5, 0.005859375, ((0, 64), (1, 2)), jnp.float32),
        "tile_cols": draw_tile_cols(jax.random.fold_in(keys[6], 71), 0),
        "tile_counts": draw_tile_counts(jax.random.fold_in(keys[6], 71), 0),
    }


def operate(field, diagonal, dense_blocks, dense_sigma, tiles, tile_cols, live, sigma):
    flat_cols = tile_cols.reshape(-1)
    partner = field[flat_cols].reshape(tile_cols.shape[0], tile_cols.shape[1], field.shape[1], field.shape[2])
    partner = partner * live[:, :, None, None]
    forward = jnp.einsum('rkab,rksb->rsa', tiles, partner, precision=lax.Precision.HIGHEST)
    forward = forward + lax.optimization_barrier(jnp.sum(sigma, axis=1))[:, None, None] * field
    back = jnp.einsum('rkab,rsa->rksb', tiles, field, precision=lax.Precision.HIGHEST) * live[:, :, None, None]
    back = back + sigma[:, :, None, None] * partner
    spread = jnp.zeros(field.shape, jnp.float32).at[flat_cols].add(back.reshape(-1, field.shape[1], field.shape[2]))
    dense_out = dense_sigma[:, None, None] * field + 0.5 * (jnp.einsum('bij,bsj->bsi', dense_blocks, field, precision=lax.Precision.HIGHEST) + jnp.einsum('bji,bsj->bsi', dense_blocks, field, precision=lax.Precision.HIGHEST))
    return forward + spread + dense_out + diagonal[:, None, :] * field

def reference(right_side, diagonal, dense_blocks, tiles, tile_cols, tile_counts):
    slot_ids = jnp.arange(tiles.shape[1], dtype=jnp.int32)
    live = (slot_ids[None, :] < tile_counts[:, None]).astype(jnp.float32)
    sigma = jnp.sqrt(lax.optimization_barrier(jnp.sum(tiles * tiles, axis=(2, 3)))) * live
    dense_sigma = jnp.sqrt(lax.optimization_barrier(jnp.sum(dense_blocks * dense_blocks, axis=(1, 2))))
    solution_field = jnp.zeros_like(right_side)
    residual, direction = (right_side, right_side)
    norm_now = lax.optimization_barrier(jnp.sum(residual * residual, axis=(0, 2)))
    for step in range(ITERS):
        image = operate(direction, diagonal, dense_blocks, dense_sigma, tiles, tile_cols, live, sigma)
        alpha = norm_now / lax.optimization_barrier(jnp.sum(direction * image, axis=(0, 2)))
        solution_field = solution_field + alpha[None, :, None] * direction
        residual = residual - alpha[None, :, None] * image
        norm_next = lax.optimization_barrier(jnp.sum(residual * residual, axis=(0, 2)))
        direction = residual + (norm_next / norm_now)[None, :, None] * direction
        norm_now = norm_next
    return (solution_field, residual)
```

```python
import functools
import jax
import jax.numpy as jnp
from jax import lax
from jax.experimental import pallas as pl
from jax.experimental.pallas import tpu as pltpu
from jax.sharding import PartitionSpec as P

MESH = pl.DeviceIdType.MESH
F32 = jnp.float32
BF16 = jnp.bfloat16
ITERS = 4
ROWS = 16
SLOTS = 4
NRHS = 8
W = 128
SLABS = 64


def split(x):
    hi = x.astype(BF16)
    return hi, (x - hi.astype(F32)).astype(BF16)


def axis_peer(s, axis, d):
    z, x, y = s // 16, (s // 4) % 4, s % 4
    if axis == 0:
        y = (y + d) % 4
    if axis == 1:
        x = (x + d) % 4
    if axis == 2:
        z = (z + d) % 4
    return z * 16 + x * 4 + y


def kernel(cols, counts, b_ref, diag_ref, dense_hbm, tiles_hbm, x_ref, r_ref,
           tf, df, wt, dw, gm, sq, sig, krylov, halo, qout, qin, pout, pin, dg, snout, snin, vs, bst,
           thout, thin, arout, arin, tile_sem, dense_sem, peer_ss, peer_rs, halo_ss, halo_rs, q_ss, q_rs, sn_ss, sn_rs, th_ss, th_rs, ar_ss, ar_rs):
    s = lax.axis_index("slab")
    c = lax.axis_index("sub")
    after = ((s + 1) % SLABS, c)
    before = ((s + SLABS - 1) % SLABS, c)
    peer = (s, 1 - c)
    first = s * ROWS

    tile_copies = [pltpu.make_async_copy(tiles_hbm.at[pl.ds(4 * i, 4)], tf.at[pl.ds(4 * i, 4)], tile_sem.at[i]) for i in range(4)]
    dense_copy = pltpu.make_async_copy(dense_hbm, df, dense_sem)
    for cp in tile_copies:
        cp.start()
    dense_copy.start()

    barrier = pltpu.get_barrier_semaphore()
    axes = [(a, d) for a in range(3) for d in (1, 2, 3)]
    for dev in [after, before, peer] + [(axis_peer(s, a, d), c) for a, d in axes]:
        pl.semaphore_signal(barrier, inc=1, device_id=dev, device_id_type=MESH)

    def remote(src, dst, ss, rs, dev):
        return pltpu.make_async_remote_copy(src_ref=src, dst_ref=dst, send_sem=ss, recv_sem=rs, device_id=dev, device_id_type=MESH)

    lane = lax.broadcasted_iota(jnp.int32, (8, W), 1)
    col_lanes = []
    for g in range(4):
        cv = jnp.zeros((8, W), jnp.int32)
        for u in range(16):
            t = g * 16 + u
            cv = jnp.where(lane // 8 == u, cols[t // SLOTS, t % SLOTS] - first, cv)
        col_lanes.append(cv)
    cv = jnp.concatenate(col_lanes, axis=1)
    sub_of = lax.broadcasted_iota(jnp.int32, (8, 512), 0)
    lane_of = lax.broadcasted_iota(jnp.int32, (8, 512), 1)
    same = lane_of % 8 == sub_of
    for j in range(0, 2 * ROWS, 2):
        top = jnp.where((cv == j) & same, 1.0, 0.0)
        low = jnp.where((cv == j + 1) & same, 1.0, 0.0)
        gm[8 * j:8 * j + 16, :] = jnp.concatenate([top, low], axis=0).astype(BF16)

    for i in range(4):
        tile_copies[i].wait()

        def prep(rr, carry):
            r = 4 * i + rr
            for k in range(SLOTS):
                live = jnp.where(c * SLOTS + k < counts[r], 1.0, 0.0).astype(F32)
                t = tf[r, k] * live
                hi, lo = split(t)
                wt[r, 0:W, W * k:W * k + W] = hi
                wt[r, W:2 * W, W * k:W * k + W] = lo
                sq[r * SLOTS + k] = jnp.sum((t * t).reshape(16, 8, W), axis=0)
            return carry

        lax.fori_loop(0, 4, prep, 0)
    total = jnp.sum(jnp.sum(sq[...], axis=2, keepdims=True), axis=1, keepdims=True)
    sigma = jnp.broadcast_to(jnp.sqrt(total), (64, 8, W))
    sig[...] = sigma
    sigma2 = sigma.reshape(512, W)
    s_hi = sigma2.astype(BF16)
    rest = sigma2 - s_hi.astype(F32)
    s_mid = rest.astype(BF16)
    s_lo = (rest - s_mid.astype(F32)).astype(BF16)
    scol = jnp.dot(gm[...], jnp.concatenate([s_hi, s_mid], axis=1), preferred_element_type=F32)
    scol = scol[:, :W] + scol[:, W:] + jnp.dot(gm[...], s_lo, preferred_element_type=F32)
    scol = scol.reshape(2 * ROWS, NRHS, W)
    snout[...] = scol[ROWS:]

    dense_copy.wait()
    dsum = jnp.zeros((8, W), F32)
    dsig = []
    for j in range(8):
        d = df[j]
        sqd = jnp.sum((d * d).reshape(16, 8, W), axis=0)
        dtot = jnp.sum(jnp.sum(sqd, axis=1, keepdims=True), axis=0, keepdims=True)
        ds = jnp.broadcast_to(jnp.sqrt(dtot), (8, W))
        dsig.append(ds)
        dsum = dsum + ds
        hi, lo = split(0.5 * (d + d.T))
        dw[j, :, 0:W] = hi
        dw[j, :, W:2 * W] = lo
    srow = jnp.sum(sig[...].reshape(ROWS, SLOTS, 8, W), axis=1)
    half = 0.5 * diag_ref[...]
    dg[...] = srow + scol[:ROWS] + half[:, None, :]
    for j in range(8):
        dg[8 * c + j] = dg[8 * c + j] + dsig[j]
    diag_sum = jnp.sum(half, axis=0, keepdims=True)
    diag_sum = jnp.sum(diag_sum, axis=1, keepdims=True)
    thout[0] = (2.0 * jnp.sum(sig[...], axis=0) + dsum) * W + diag_sum

    pl.semaphore_wait(barrier, 12)

    sn_copy = remote(snout, snin, sn_ss, sn_rs, after)
    theta_peer = remote(thout.at[0], thin.at[0], th_ss.at[0], th_rs.at[0], peer)
    theta_peer.start()

    def reduce_phase(phase, out, into, ss, rs):
        return [remote(out.at[1 + phase], into.at[1 + 3 * phase + d - 1], ss.at[1 + 3 * phase + d - 1], rs.at[1 + 3 * phase + d - 1],
                       (axis_peer(s, phase, d), c)) for d in (1, 2, 3)]

    theta_phases = [reduce_phase(a, thout, thin, th_ss, th_rs) for a in range(3)]
    final_phases = [reduce_phase(a, arout, arin, ar_ss, ar_rs) for a in range(3)]

    def theta_step(n):
        if n == 0:
            theta_peer.wait_recv()
            thout[1] = thout[0] + thin[0]
        else:
            for cp in theta_phases[n - 1]:
                cp.wait_recv()
            k = 1 + 3 * (n - 1)
            thout[1 + n] = thout[n] + ((thin[k] + thin[k + 1]) + thin[k + 2])
        if n < 3:
            for cp in theta_phases[n]:
                cp.start()

    def lanes_sum(x):
        return jnp.sum(x, axis=1, keepdims=True)

    def inner(x, y):
        return jnp.broadcast_to(lanes_sum(jnp.sum(x * y, axis=0)), (8, W))

    krylov[0] = b_ref[...]
    lane8 = lax.broadcasted_iota(jnp.int32, (8, W), 1)
    moments = jnp.zeros((8, W), F32)
    theta = None
    halo_copies, q_copies, p_copies = [], [], []
    for t in range(ITERS):
        hc = remote(krylov.at[t], halo.at[t], halo_ss.at[t], halo_rs.at[t], before)
        hc.start()
        halo_copies.append(hc)
        for j in range(ROWS):
            hi, lo = split(krylov[t, j])
            vs[j] = jnp.concatenate([hi.astype(F32), lo.astype(F32)], axis=0).astype(BF16)
        for r in range(ROWS):
            y = vs[r]
            out = jnp.dot(jnp.concatenate([y, y], axis=1), wt[r], preferred_element_type=F32)
            out = out[0:8] + out[8:16]
            for h in range(2):
                pair = jnp.concatenate([out[:, 256 * h:256 * h + W], out[:, 256 * h + W:256 * h + 2 * W]], axis=0)
                hi, lo = split(pair)
                at = (r * SLOTS + 2 * h) * 8
                bst[at:at + 16, 0:W] = hi
                bst[at:at + 16, W:2 * W] = lo
        spread = jnp.dot(gm[...], bst[...], preferred_element_type=F32)
        spread = (spread[:, :W] + spread[:, W:]).reshape(2 * ROWS, NRHS, W)
        qout[t] = spread[ROWS:]
        qc = remote(qout.at[t], qin.at[t], q_ss.at[t], q_rs.at[t], after)
        qc.start()
        q_copies.append(qc)
        if t == 0:
            sn_copy.start()
        pout[t] = spread[:ROWS] + dg[...] * krylov[t]
        for j in range(8):
            out = jnp.dot(vs[8 * c + j], dw[j], preferred_element_type=F32)
            out = out[0:8] + out[8:16]
            pout[t, 8 * c + j] = pout[t, 8 * c + j] + (out[:, :W] + out[:, W:])
        if t < 2:
            theta_step(2 * t)
        hc.wait_recv()
        for j in range(ROWS):
            hi, lo = split(halo[t, j])
            vs[ROWS + j] = jnp.concatenate([hi.astype(F32), lo.astype(F32)], axis=0).astype(BF16)
        for r in range(ROWS):
            x = jnp.concatenate([vs[jnp.clip(cols[r, k] - first, 0, 2 * ROWS - 1)] for k in range(SLOTS)], axis=1)
            out = lax.dot_general(x, wt[r], (((1,), (1,)), ((), ())), preferred_element_type=F32)
            out = out[0:8] + out[8:16]
            pout[t, r] = pout[t, r] + (out[:, :W] + out[:, W:])
        if t == 0:
            sn_copy.wait_recv()
            dg[...] = dg[...] + snin[...]
            pout[t] = pout[t] + snin[...] * krylov[t]
        qc.wait_recv()
        pout[t] = pout[t] + qin[t]
        pc = remote(pout.at[t], pin.at[t], peer_ss.at[t], peer_rs.at[t], peer)
        pc.start()
        p_copies.append(pc)
        if t < 2:
            theta_step(2 * t + 1)
        if t == 1:
            theta = thout[4] * (1.0 / (SLABS * ROWS * W))
        pc.wait_recv()
        image = pout[t] + pin[t]
        if t == 0:
            krylov[1] = image
        elif t == 1:
            hc.wait_send()
            plain = krylov[1]
            one = plain - theta * krylov[0]
            krylov[1] = one
            krylov[2] = image - theta * (plain + one)
            pairs = [(0, 0), (0, 1), (1, 1), (1, 2), (2, 2)]
        else:
            krylov[t + 1] = image - theta * krylov[t]
            pairs = [(t, t + 1), (t + 1, t + 1)][:1 if t == 3 else 2]
        if t >= 1:
            for i, j in pairs:
                moments = jnp.where(lane8 == i + j, inner(krylov[i], krylov[j]), moments)

    arout[1] = moments
    for a in range(3):
        for cp in final_phases[a]:
            cp.start()
        for cp in final_phases[a]:
            cp.wait_recv()
        k = 1 + 3 * a
        arout[2 + a] = arout[1 + a] + ((arin[k] + arin[k + 1]) + arin[k + 2])
    summed = arout[4]
    m = [jnp.broadcast_to(summed[:, k:k + 1], (8, W)) for k in range(8)]

    def dot(p, q):
        n = {}
        for i, u in enumerate(p):
            for j, v in enumerate(q):
                n[i + j] = n[i + j] + u * v if i + j in n else u * v
        total = None
        for k, u in n.items():
            total = u * m[k] if total is None else total + u * m[k]
        return total

    one = jnp.ones((8, W), F32)
    res, direction, sol = [one], [one], []
    rr = m[0]
    for it in range(ITERS):
        n = len(direction)
        image = [theta * direction[0]] + [direction[i - 1] + theta * direction[i] for i in range(1, n)] + [direction[-1]]
        alpha = rr / dot(direction, image)
        sol = [(sol[i] + alpha * direction[i]) if i < len(sol) else alpha * direction[i] for i in range(n)]
        res = [(res[i] - alpha * image[i]) if i < len(res) else -alpha * image[i] for i in range(n + 1)]
        if it < ITERS - 1:
            new = dot(res, res)
            beta = new / rr
            direction = [(res[i] + beta * direction[i]) if i < n else res[i] for i in range(n + 1)]
            rr = new
    xs = sol[0] * krylov[0]
    rs = res[0] * krylov[0]
    for i in range(1, ITERS + 1):
        if i < ITERS:
            xs = xs + sol[i] * krylov[i]
        rs = rs + res[i] * krylov[i]
    x_ref[...] = xs
    r_ref[...] = rs

    sn_copy.wait_send()
    theta_peer.wait_send()
    for ph in theta_phases + final_phases:
        for cp in ph:
            cp.wait_send()
    for t in range(ITERS):
        if t != 1:
            halo_copies[t].wait_send()
        q_copies[t].wait_send()
        p_copies[t].wait_send()


def body(right_side, diagonal, dense_blocks, tiles, tile_cols, tile_counts):
    vmem = pl.BlockSpec(memory_space=pltpu.VMEM)
    smem = pl.BlockSpec(memory_space=pltpu.SMEM)
    anym = pl.BlockSpec(memory_space=pl.ANY)
    vec = (ROWS, NRHS, W)
    dma = pltpu.SemaphoreType.DMA
    out = jax.ShapeDtypeStruct(vec, F32)
    return pl.pallas_call(
        kernel,
        out_shape=(out, out),
        in_specs=[smem, smem, vmem, vmem, anym, anym],
        out_specs=(vmem, vmem),
        scratch_shapes=[
            pltpu.VMEM((ROWS, SLOTS, W, W), F32),
            pltpu.VMEM((8, W, W), F32),
            pltpu.VMEM((ROWS, 2 * W, SLOTS * W), BF16),
            pltpu.VMEM((8, W, 2 * W), BF16),
            pltpu.VMEM((2 * ROWS * NRHS, 512), BF16),
            pltpu.VMEM((64, 8, W), F32),
            pltpu.VMEM((64, 8, W), F32),
            pltpu.VMEM((ITERS + 1,) + vec, F32),
            pltpu.VMEM((ITERS,) + vec, F32),
            pltpu.VMEM((ITERS,) + vec, F32),
            pltpu.VMEM((ITERS,) + vec, F32),
            pltpu.VMEM((ITERS,) + vec, F32),
            pltpu.VMEM((ITERS,) + vec, F32),
            pltpu.VMEM(vec, F32),
            pltpu.VMEM(vec, F32),
            pltpu.VMEM(vec, F32),
            pltpu.VMEM((2 * ROWS, 16, W), BF16),
            pltpu.VMEM((512, 2 * W), BF16),
            pltpu.VMEM((5, 8, W), F32),
            pltpu.VMEM((10, 8, W), F32),
            pltpu.VMEM((5, 8, W), F32),
            pltpu.VMEM((10, 8, W), F32),
            dma((4,)),
            dma,
            dma((ITERS,)),
            dma((ITERS,)),
            dma((ITERS,)),
            dma((ITERS,)),
            dma((ITERS,)),
            dma((ITERS,)),
            dma,
            dma,
            dma((10,)),
            dma((10,)),
            dma((10,)),
            dma((10,)),
        ],
        compiler_params=pltpu.CompilerParams(collective_id=0, has_side_effects=True, vmem_limit_bytes=40 << 20),
    )(tile_cols, tile_counts, right_side, diagonal, dense_blocks, tiles)


def solution(mesh):
    return jax.shard_map(
        body,
        mesh=mesh,
        in_specs=(
            P("slab", None, None),
            P("slab", None),
            P(("slab", "sub"), None, None),
            P("slab", "sub", None, None),
            P("slab", "sub"),
            P("slab"),
        ),
        out_specs=(P("slab", None, None), P("slab", None, None)),
        check_vma=False,
    )
```

```python
import functools
import jax
import jax.numpy as jnp
from jax import lax
from jax.experimental import pallas as pl
from jax.experimental.pallas import tpu as pltpu
from jax.sharding import PartitionSpec as P

MESH = pl.DeviceIdType.MESH
F32 = jnp.float32
BF16 = jnp.bfloat16
ITERS = 4
ROWS = 16
SLOTS = 4
NRHS = 8
W = 128
SLABS = 64


def split(x):
    hi = x.astype(BF16)
    return hi, (x - hi.astype(F32)).astype(BF16)


def kernel(cols_hbm, counts_hbm, b_hbm, diag_hbm, dense_hbm, tiles_hbm, x_ref, r_ref,
           cols, counts, diag_ref, tf, df, wt, dw, gm, sq, krylov, halo, qout, qin, pout, pin, dg, snout, snin, vs, bst,
           pair_out, pair_in, all_in, in_sem, tile_sem, peer_ss, peer_rs, halo_ss, halo_rs, q_ss, q_rs, sn_ss, sn_rs, pair_ss, pair_rs, all_ss, all_rs):
    s = lax.axis_index("slab")
    c = lax.axis_index("sub")
    after = ((s + 1) % SLABS, c)
    before = ((s + SLABS - 1) % SLABS, c)
    peer = (s, 1 - c)
    first = s * ROWS

    small_copies = [pltpu.make_async_copy(a, b, in_sem.at[i]) for i, (a, b) in enumerate(
        [(cols_hbm, cols), (counts_hbm, counts), (b_hbm, krylov.at[0]), (diag_hbm, diag_ref), (dense_hbm, df)])]
    tile_copies = [pltpu.make_async_copy(tiles_hbm.at[pl.ds(4 * i, 4)], tf.at[pl.ds(4 * i, 4)], tile_sem.at[i]) for i in range(4)]
    for cp in small_copies[:3] + tile_copies + small_copies[3:]:
        cp.start()

    barrier = pltpu.get_barrier_semaphore()
    pl.semaphore_signal(barrier, inc=1, device_id=peer, device_id_type=MESH)

    def greet(d, carry):
        pl.semaphore_signal(barrier, inc=1, device_id=((s + d) % SLABS, c), device_id_type=MESH)
        return carry

    lax.fori_loop(1, SLABS, greet, 0, unroll=True)

    def remote(src, dst, ss, rs, dev):
        return pltpu.make_async_remote_copy(src_ref=src, dst_ref=dst, send_sem=ss, recv_sem=rs, device_id=dev, device_id_type=MESH)

    small_copies[0].wait()
    small_copies[1].wait()
    lane = lax.broadcasted_iota(jnp.int32, (8, W), 1)
    col_lanes = []
    for g in range(4):
        cv = jnp.zeros((8, W), jnp.int32)
        for u in range(16):
            t = g * 16 + u
            cv = jnp.where(lane // 8 == u, cols[t % SLOTS, t // SLOTS] - first, cv)
        col_lanes.append(cv)
    cv = jnp.concatenate(col_lanes, axis=1)
    sub_of = lax.broadcasted_iota(jnp.int32, (8, 512), 0)
    lane_of = lax.broadcasted_iota(jnp.int32, (8, 512), 1)
    cv = jnp.where(lane_of % 8 == sub_of, cv, -1)
    for j in range(0, 2 * ROWS, 2):
        top = jnp.where(cv == j, 1.0, 0.0)
        low = jnp.where(cv == j + 1, 1.0, 0.0)
        gm[8 * j:8 * j + 16, :] = jnp.concatenate([top, low], axis=0).astype(BF16)

    def own_parts(t):
        for j in range(ROWS):
            hi, lo = split(krylov[t, j])
            vs[j] = jnp.concatenate([hi.astype(F32), lo.astype(F32)], axis=0).astype(BF16)

    small_copies[2].wait()
    own_parts(0)

    for i in range(4):
        tile_copies[i].wait()

        def prep(rr, carry):
            r = 4 * i + rr
            for k in range(SLOTS):
                live = jnp.where(c * SLOTS + k < counts[r], 1.0, 0.0).astype(F32)
                t = tf[r, k] * live
                hi, lo = split(t)
                wt[r, 0:W, W * k:W * k + W] = hi
                wt[r, W:2 * W, W * k:W * k + W] = lo
                sq[r * SLOTS + k] = jnp.sum((t * t).reshape(16, 8, W), axis=0)
            return carry

        lax.fori_loop(0, 4, prep, 0, unroll=True)

    pl.semaphore_wait(barrier, SLABS)

    def spread_q(t):
        for r in range(ROWS):
            y = vs[r]
            out = jnp.dot(jnp.concatenate([y, y], axis=1), wt[r], preferred_element_type=F32)
            out = out[0:8] + out[8:16]
            for h in range(2):
                pair = jnp.concatenate([out[:, 256 * h:256 * h + W], out[:, 256 * h + W:256 * h + 2 * W]], axis=0)
                hi, lo = split(pair)
                at = (r * SLOTS + 2 * h) * 8
                bst[at:at + 16, 0:W] = hi
                bst[at:at + 16, W:2 * W] = lo
        spread = jnp.dot(gm[...], bst[...], preferred_element_type=F32)
        spread = (spread[:, :W] + spread[:, W:]).reshape(2 * ROWS, NRHS, W)
        qout[t] = spread[ROWS:]
        pout[t] = spread[:ROWS]

    halo_copies = [remote(krylov.at[t], halo.at[t], halo_ss.at[t], halo_rs.at[t], before) for t in range(ITERS)]
    q_copies = [remote(qout.at[t], qin.at[t], q_ss.at[t], q_rs.at[t], after) for t in range(ITERS)]
    p_copies = [remote(pout.at[t], pin.at[t], peer_ss.at[t], peer_rs.at[t], peer) for t in range(ITERS)]
    sn_copy = remote(snout, snin, sn_ss, sn_rs, after)
    pair_copies = [remote(pair_out.at[i], pair_in.at[i], pair_ss.at[i], pair_rs.at[i], peer) for i in range(2)]

    def all_start(i):
        pair_copies[i].wait_recv()
        pair_out[2 + i, 0:1] = pair_out[i, 0:1] + pair_in[i, 0:1]

        def send(d, carry):
            remote(pair_out.at[2 + i, pl.ds(0, 1)], all_in.at[i, d - 1], all_ss.at[i], all_rs.at[i], ((s + d) % SLABS, c)).start()
            return carry

        lax.fori_loop(1, SLABS, send, 0, unroll=True)

    def all_copy(i):
        return remote(all_in.at[i], all_in.at[i], all_ss.at[i], all_rs.at[i], peer)

    def all_done(i):
        all_copy(i).wait_recv()
        return pair_out[2 + i, 0:1] + jnp.sum(all_in[i], axis=0)

    halo_copies[0].start()
    spread_q(0)
    q_copies[0].start()

    sigma = jnp.broadcast_to(jnp.sqrt(jnp.sum(jnp.sum(sq[...], axis=2, keepdims=True), axis=1, keepdims=True)), (64, 8, W))
    sigma2 = sigma.reshape(512, W)
    s_hi = sigma2.astype(BF16)
    rest = sigma2 - s_hi.astype(F32)
    s_mid = rest.astype(BF16)
    s_lo = (rest - s_mid.astype(F32)).astype(BF16)
    scol = jnp.dot(gm[...], jnp.concatenate([s_hi, s_mid], axis=1), preferred_element_type=F32)
    scol = scol[:, :W] + scol[:, W:] + jnp.dot(gm[...], s_lo, preferred_element_type=F32)
    scol = scol.reshape(2 * ROWS, NRHS, W)
    snout[...] = scol[ROWS:]
    sn_copy.start()

    small_copies[3].wait()
    small_copies[4].wait()
    dsum = jnp.zeros((8, W), F32)
    dsig = []
    for j in range(8):
        d = df[j]
        sqd = jnp.sum((d * d).reshape(16, 8, W), axis=0)
        dtot = jnp.sum(jnp.sum(sqd, axis=1, keepdims=True), axis=0, keepdims=True)
        ds = jnp.broadcast_to(jnp.sqrt(dtot), (8, W))
        dsig.append(ds)
        dsum = dsum + ds
    half = 0.5 * diag_ref[...]
    diag_sum = jnp.sum(jnp.sum(half, axis=0, keepdims=True), axis=1, keepdims=True)
    pair_out[0] = (2.0 * jnp.sum(sigma, axis=0) + dsum) * W + diag_sum
    pair_copies[0].start()
    for j in range(8):
        d = df[j]
        hi, lo = split(0.5 * (d + d.T))
        dw[j, :, 0:W] = hi
        dw[j, :, W:2 * W] = lo
    dg[...] = jnp.sum(sigma.reshape(ROWS, SLOTS, 8, W), axis=1) + scol[:ROWS] + half[:, None, :]
    for j in range(8):
        dg[8 * c + j] = dg[8 * c + j] + dsig[j]

    sub8 = lax.broadcasted_iota(jnp.int32, (8, W), 0)

    def place(k, x, row):
        return jnp.where(lane == 8 * sub8 + k, jnp.sum(x, axis=1, keepdims=True), row)

    def inner(i, j):
        return jnp.sum(krylov[i] * krylov[j], axis=0)

    def local_part(t):
        loc = [dg[r] * krylov[t, r] for r in range(ROWS)]
        for r in range(ROWS):
            pout[t, r] = pout[t, r] + loc[r]
        seen = loc[0] * krylov[t, 0]
        for r in range(1, ROWS):
            seen = seen + loc[r] * krylov[t, r]
        for j in range(8):
            out = jnp.dot(vs[8 * c + j], dw[j], preferred_element_type=F32)
            out = out[0:8] + out[8:16]
            out = out[:, :W] + out[:, W:]
            pout[t, 8 * c + j] = pout[t, 8 * c + j] + out
            seen = seen + out * krylov[t, 8 * c + j]
        return seen

    def forward(t):
        for j in range(ROWS):
            hi, lo = split(halo[t, j])
            vs[ROWS + j] = jnp.concatenate([hi.astype(F32), lo.astype(F32)], axis=0).astype(BF16)
        seen = jnp.zeros((8, W), F32)
        for r in range(ROWS):
            x = jnp.concatenate([vs[jnp.clip(cols[k, r] - first, 0, 2 * ROWS - 1)] for k in range(SLOTS)], axis=1)
            out = lax.dot_general(x, wt[r], (((1,), (1,)), ((), ())), preferred_element_type=F32)
            out = out[0:8] + out[8:16]
            out = out[:, :W] + out[:, W:]
            pout[t, r] = pout[t, r] + out
            seen = seen + out * krylov[t, r]
        return seen

    moments = jnp.zeros((8, W), F32)
    theta = None
    for t in range(ITERS):
        if t > 0:
            halo_copies[t].start()
            own_parts(t)
            spread_q(t)
            q_copies[t].start()
        seen = local_part(t)
        if t == 2:
            for i, j in [(0, 0), (0, 1), (1, 1), (1, 2), (2, 2)]:
                moments = place(i + j, inner(i, j), moments)
        if t == 3:
            for i, j in [(2, 3), (3, 3)]:
                moments = place(i + j, inner(i, j), moments)
        if t == 0:
            all_start(0)
        halo_copies[t].wait_recv()
        crossed = forward(t)
        if t == 3:
            row = 0.5 * moments + place(7, seen + 2.0 * crossed, jnp.zeros((8, W), F32))
            pair_out[1] = jnp.broadcast_to(jnp.sum(row, axis=0, keepdims=True), (8, W))
            pair_copies[1].start()
        if t == 0:
            sn_copy.wait_recv()
            dg[...] = dg[...] + snin[...]
            pout[t] = pout[t] + snin[...] * krylov[t]
        q_copies[t].wait_recv()
        pout[t] = pout[t] + qin[t]
        p_copies[t].start()
        if t == 3:
            all_start(1)
        if t == 1:
            theta = jnp.broadcast_to(all_done(0) * (1.0 / (SLABS * ROWS * W)), (8, W))
            dg[...] = dg[...] - 0.5 * theta
        p_copies[t].wait_recv()
        image = pout[t] + pin[t]
        if t == 1:
            halo_copies[1].wait_send()
            plain = krylov[1]
            one = plain - theta * krylov[0]
            krylov[1] = one
            krylov[2] = image - theta * (plain + one)
        else:
            krylov[t + 1] = image

    summed = jnp.broadcast_to(all_done(1), (8, W))
    m = [jnp.broadcast_to(jnp.sum(jnp.where(lane == 8 * sub8 + k, summed, 0.0), axis=1, keepdims=True), (8, W)) for k in range(8)]

    def dot(p, q):
        n = {}
        for i, u in enumerate(p):
            for j, v in enumerate(q):
                n[i + j] = n[i + j] + u * v if i + j in n else u * v
        total = None
        for k, u in n.items():
            total = u * m[k] if total is None else total + u * m[k]
        return total

    one = jnp.ones((8, W), F32)
    res, direction, sol = [one], [one], []
    rr = m[0]
    for it in range(ITERS):
        n = len(direction)
        image = [theta * direction[0]] + [direction[i - 1] + theta * direction[i] for i in range(1, n)] + [direction[-1]]
        alpha = rr / dot(direction, image)
        sol = [(sol[i] + alpha * direction[i]) if i < len(sol) else alpha * direction[i] for i in range(n)]
        res = [(res[i] - alpha * image[i]) if i < len(res) else -alpha * image[i] for i in range(n + 1)]
        if it < ITERS - 1:
            new = dot(res, res)
            beta = new / rr
            direction = [(res[i] + beta * direction[i]) if i < n else res[i] for i in range(n + 1)]
            rr = new
    for j in range(ROWS):
        xs = sol[0] * krylov[0, j]
        rs = res[0] * krylov[0, j]
        for i in range(1, ITERS + 1):
            if i < ITERS:
                xs = xs + sol[i] * krylov[i, j]
            rs = rs + res[i] * krylov[i, j]
        x_ref[j] = xs
        r_ref[j] = rs

    sn_copy.wait_send()
    for i in range(2):
        pair_copies[i].wait_send()
        all_copy(i).wait_send()
    for t in range(ITERS):
        if t != 1:
            halo_copies[t].wait_send()
        q_copies[t].wait_send()
        p_copies[t].wait_send()


def body(right_side, diagonal, dense_blocks, tiles, tile_cols, tile_counts):
    vmem = pl.BlockSpec(memory_space=pltpu.VMEM)
    anym = pl.BlockSpec(memory_space=pl.ANY)
    vec = (ROWS, NRHS, W)
    dma = pltpu.SemaphoreType.DMA
    out = jax.ShapeDtypeStruct(vec, F32)
    return pl.pallas_call(
        kernel,
        out_shape=(out, out),
        in_specs=[anym] * 6,
        out_specs=(vmem, vmem),
        scratch_shapes=[
            pltpu.SMEM((SLOTS, ROWS), jnp.int32),
            pltpu.SMEM((ROWS,), jnp.int32),
            pltpu.VMEM((ROWS, W), F32),
            pltpu.VMEM((ROWS, SLOTS, W, W), F32),
            pltpu.VMEM((8, W, W), F32),
            pltpu.VMEM((ROWS, 2 * W, SLOTS * W), BF16),
            pltpu.VMEM((8, W, 2 * W), BF16),
            pltpu.VMEM((2 * ROWS * NRHS, 512), BF16),
            pltpu.VMEM((64, 8, W), F32),
            pltpu.VMEM((ITERS + 1,) + vec, F32),
            pltpu.VMEM((ITERS,) + vec, F32),
            pltpu.VMEM((ITERS,) + vec, F32),
            pltpu.VMEM((ITERS,) + vec, F32),
            pltpu.VMEM((ITERS,) + vec, F32),
            pltpu.VMEM((ITERS,) + vec, F32),
            pltpu.VMEM(vec, F32),
            pltpu.VMEM(vec, F32),
            pltpu.VMEM(vec, F32),
            pltpu.VMEM((2 * ROWS, 16, W), BF16),
            pltpu.VMEM((512, 2 * W), BF16),
            pltpu.VMEM((4, 8, W), F32),
            pltpu.VMEM((2, 8, W), F32),
            pltpu.VMEM((2, SLABS - 1, 1, W), F32),
            dma((5,)),
            dma((4,)),
            dma((ITERS,)),
            dma((ITERS,)),
            dma((ITERS,)),
            dma((ITERS,)),
            dma((ITERS,)),
            dma((ITERS,)),
            dma,
            dma,
            dma((2,)),
            dma((2,)),
            dma((2,)),
            dma((2,)),
        ],
        compiler_params=pltpu.CompilerParams(collective_id=0, has_side_effects=True, vmem_limit_bytes=60 << 20),
    )(tile_cols.T, tile_counts, right_side, diagonal, dense_blocks, tiles)


def solution(mesh):
    return jax.shard_map(
        body,
        mesh=mesh,
        in_specs=(
            P("slab", None, None),
            P("slab", None),
            P(("slab", "sub"), None, None),
            P("slab", "sub", None, None),
            P("slab", "sub"),
            P("slab"),
        ),
        out_specs=(P("slab", None, None), P("slab", None, None)),
        check_vma=False,
    )
```

```python
import functools
import jax
import jax.numpy as jnp
from jax import lax
from jax.experimental import pallas as pl
from jax.experimental.pallas import tpu as pltpu
from jax.sharding import PartitionSpec as P

MESH = pl.DeviceIdType.MESH
F32 = jnp.float32
BF16 = jnp.bfloat16
ITERS = 4
ROWS = 16
SLOTS = 4
NRHS = 8
W = 128
SLABS = 64


def split(x):
    hi = x.astype(BF16)
    return hi, (x - hi.astype(F32)).astype(BF16)


def kernel(cols_hbm, counts_hbm, b_hbm, diag_hbm, dense_hbm, tiles_hbm, basis_hbm, sol_ref, res_ref,
           cols, counts, diag_ref, tf, df, wt, wf, dw, gm, sq, krylov, halo, qout, qin, pout, pin, dg, snout, snin, vs, bst,
           pair_out, pair_in, all_in, in_sem, out_sem, tile_sem, peer_ss, peer_rs, halo_ss, halo_rs, q_ss, q_rs, sn_ss, sn_rs, pair_ss, pair_rs, all_ss, all_rs):
    s = lax.axis_index("slab")
    c = lax.axis_index("sub")
    after = ((s + 1) % SLABS, 1 - c)
    before = ((s + SLABS - 1) % SLABS, 1 - c)
    peer = (s, 1 - c)
    first = s * ROWS

    small_copies = [pltpu.make_async_copy(a, b, in_sem.at[i]) for i, (a, b) in enumerate(
        [(cols_hbm, cols), (counts_hbm, counts), (b_hbm, krylov.at[0]), (diag_hbm, diag_ref), (dense_hbm, df)])]
    tile_copies = [pltpu.make_async_copy(tiles_hbm.at[pl.ds(4 * i, 4)], tf.at[pl.ds(4 * i, 4)], tile_sem.at[i]) for i in range(4)]
    for cp in small_copies[:3] + tile_copies + small_copies[3:]:
        cp.start()

    barrier = pltpu.get_barrier_semaphore()
    for dev in (peer, after, before):
        pl.semaphore_signal(barrier, inc=1, device_id=dev, device_id_type=MESH)

    def greet(d, carry):
        pl.semaphore_signal(barrier, inc=1, device_id=((s + d) % SLABS, c), device_id_type=MESH)
        return carry

    lax.fori_loop(1, SLABS, greet, 0, unroll=True)

    def remote(src, dst, ss, rs, dev):
        return pltpu.make_async_remote_copy(src_ref=src, dst_ref=dst, send_sem=ss, recv_sem=rs, device_id=dev, device_id_type=MESH)

    small_copies[0].wait()
    small_copies[1].wait()
    lane = lax.broadcasted_iota(jnp.int32, (8, W), 1)
    col_lanes = []
    for g in range(4):
        cv = jnp.zeros((8, W), jnp.int32)
        for u in range(16):
            t = g * 16 + u
            cv = jnp.where(lane // 8 == u, cols[t % SLOTS, t // SLOTS] - first, cv)
        col_lanes.append(cv)
    cv = jnp.concatenate(col_lanes, axis=1)
    sub_of = lax.broadcasted_iota(jnp.int32, (8, 512), 0)
    lane_of = lax.broadcasted_iota(jnp.int32, (8, 512), 1)
    cv = jnp.where(lane_of % 8 == sub_of, cv, -1)
    for j in range(0, 2 * ROWS, 2):
        top = jnp.where(cv == j, 1.0, 0.0)
        low = jnp.where(cv == j + 1, 1.0, 0.0)
        gm[8 * j:8 * j + 16, :] = jnp.concatenate([top, low], axis=0).astype(BF16)

    def own_parts(t):
        for j in range(ROWS):
            hi, lo = split(krylov[t, j])
            vs[j] = jnp.concatenate([hi.astype(F32), lo.astype(F32)], axis=0).astype(BF16)

    small_copies[2].wait()
    own_parts(0)

    def back(r):
        y = vs[r]
        out = jnp.dot(jnp.concatenate([y, y], axis=1), wt[r], preferred_element_type=F32)
        out = out[0:8] + out[8:16]
        for h in range(2):
            pair = jnp.concatenate([out[:, 256 * h:256 * h + W], out[:, 256 * h + W:256 * h + 2 * W]], axis=0)
            hi, lo = split(pair)
            at = (r * SLOTS + 2 * h) * 8
            bst[at:at + 16, 0:W] = hi
            bst[at:at + 16, W:2 * W] = lo

    def spread_q(t):
        spread = jnp.dot(gm[...], bst[...], preferred_element_type=F32)
        spread = (spread[:, :W] + spread[:, W:]).reshape(2 * ROWS, NRHS, W)
        qout[t] = spread[ROWS:]
        pout[t] = spread[:ROWS]

    for i in range(4):
        tile_copies[i].wait()
        for r in range(4 * i, 4 * i + 4):
            for k in range(SLOTS):
                live = jnp.where(c * SLOTS + k < counts[r], 1.0, 0.0).astype(F32)
                t = tf[r, k] * live
                hi, lo = split(t)
                wt[r, 0:W, W * k:W * k + W] = hi
                wt[r, W:2 * W, W * k:W * k + W] = lo
                sq[r * SLOTS + k] = jnp.sum((t * t).reshape(16, 8, W), axis=0)
            back(r)
    spread_q(0)
    pl.semaphore_wait(barrier, SLABS + 2)

    halo_copies = [remote(krylov.at[t], halo.at[t], halo_ss.at[t], halo_rs.at[t], before) for t in range(ITERS)]
    q_copies = [remote(qout.at[t], qin.at[t], q_ss.at[t], q_rs.at[t], after) for t in range(ITERS)]
    p_copies = [remote(pout.at[t], pin.at[t], peer_ss.at[t], peer_rs.at[t], peer) for t in range(ITERS)]
    sn_copy = remote(snout, snin, sn_ss, sn_rs, after)
    pair_copies = [remote(pair_out.at[i], pair_in.at[i], pair_ss.at[i], pair_rs.at[i], peer) for i in range(2)]

    def all_start(i):
        pair_copies[i].wait_recv()
        pair_out[2 + i, 0:1] = pair_out[i, 0:1] + pair_in[i, 0:1]

        def send(d, carry):
            remote(pair_out.at[2 + i, pl.ds(0, 1)], all_in.at[i, d - 1], all_ss.at[i], all_rs.at[i], ((s + d) % SLABS, c)).start()
            return carry

        lax.fori_loop(1, SLABS, send, 0, unroll=True)

    def all_copy(i):
        return remote(all_in.at[i], all_in.at[i], all_ss.at[i], all_rs.at[i], peer)

    def all_done(i):
        all_copy(i).wait_recv()
        return pair_out[2 + i, 0:1] + jnp.sum(all_in[i], axis=0)

    halo_copies[0].start()
    q_copies[0].start()

    sigma = jnp.broadcast_to(jnp.sqrt(jnp.sum(jnp.sum(sq[...], axis=2, keepdims=True), axis=1, keepdims=True)), (64, 8, W))
    sigma2 = sigma.reshape(512, W)
    s_hi = sigma2.astype(BF16)
    rest = sigma2 - s_hi.astype(F32)
    s_mid = rest.astype(BF16)
    s_lo = (rest - s_mid.astype(F32)).astype(BF16)
    scol = jnp.dot(gm[...], jnp.concatenate([s_hi, s_mid], axis=1), preferred_element_type=F32)
    scol = scol[:, :W] + scol[:, W:] + jnp.dot(gm[...], s_lo, preferred_element_type=F32)
    scol = scol.reshape(2 * ROWS, NRHS, W)
    snout[...] = scol[ROWS:]
    sn_copy.start()

    small_copies[3].wait()
    small_copies[4].wait()
    dsum = jnp.zeros((8, W), F32)
    dsig = []
    for j in range(8):
        d = df[j]
        sqd = jnp.sum((d * d).reshape(16, 8, W), axis=0)
        dtot = jnp.sum(jnp.sum(sqd, axis=1, keepdims=True), axis=0, keepdims=True)
        ds = jnp.broadcast_to(jnp.sqrt(dtot), (8, W))
        dsig.append(ds)
        dsum = dsum + ds
    half = 0.5 * diag_ref[...]
    diag_sum = jnp.sum(jnp.sum(half, axis=0, keepdims=True), axis=1, keepdims=True)
    pair_out[0] = (2.0 * jnp.sum(sigma, axis=0) + dsum) * W + diag_sum
    pair_copies[0].start()
    for j in range(8):
        d = df[j]
        hi, lo = split(0.5 * (d + d.T))
        dw[j, :, 0:W] = hi
        dw[j, :, W:2 * W] = lo
    dg[...] = jnp.sum(sigma.reshape(ROWS, SLOTS, 8, W), axis=1) + scol[:ROWS] + half[:, None, :]
    for j in range(8):
        dg[8 * c + j] = dg[8 * c + j] + dsig[j]

    sub8 = lax.broadcasted_iota(jnp.int32, (8, W), 0)

    def place(k, x, row):
        return jnp.where(lane == 8 * sub8 + k, jnp.sum(x, axis=1, keepdims=True), row)

    def inner(i, j):
        return jnp.sum(krylov[i] * krylov[j], axis=0)

    def local_part(t):
        loc = [dg[r] * krylov[t, r] for r in range(ROWS)]
        for r in range(ROWS):
            pout[t, r] = pout[t, r] + loc[r]
        seen = loc[0] * krylov[t, 0]
        for r in range(1, ROWS):
            seen = seen + loc[r] * krylov[t, r]
        for j in range(8):
            out = jnp.dot(vs[8 * c + j], dw[j], preferred_element_type=F32)
            out = out[0:8] + out[8:16]
            out = out[:, :W] + out[:, W:]
            pout[t, 8 * c + j] = pout[t, 8 * c + j] + out
            seen = seen + out * krylov[t, 8 * c + j]
        return seen

    def forward(t):
        for j in range(ROWS):
            hi, lo = split(halo[t, j])
            vs[ROWS + j] = jnp.concatenate([hi.astype(F32), lo.astype(F32)], axis=0).astype(BF16)
        seen = jnp.zeros((8, W), F32)
        for r in range(ROWS):
            x = jnp.concatenate([vs[jnp.clip(cols[k, r] - first, 0, 2 * ROWS - 1)] for k in range(SLOTS)], axis=1)
            out = jnp.dot(x, wf[r], preferred_element_type=F32)
            out = out[0:8] + out[8:16]
            out = out[:, :W] + out[:, W:]
            pout[t, r] = pout[t, r] + out
            seen = seen + out * krylov[t, r]
        return seen

    basis_copies = [pltpu.make_async_copy(krylov.at[i], basis_hbm.at[i], out_sem.at[i]) for i in range(ITERS + 1)]
    moments = jnp.zeros((8, W), F32)
    theta = None
    for t in range(ITERS):
        if t > 0:
            halo_copies[t].start()
            own_parts(t)
            for r in range(ROWS):
                back(r)
            spread_q(t)
            q_copies[t].start()
        seen = local_part(t)
        if t == 2:
            for i, j in [(0, 0), (0, 1), (1, 1), (1, 2), (2, 2)]:
                moments = place(i + j, inner(i, j), moments)
        if t == 3:
            for i, j in [(2, 3), (3, 3)]:
                moments = place(i + j, inner(i, j), moments)
        if t == 0:
            for r in range(8):
                wf[r] = wt[r].T
            all_start(0)
            for r in range(8, ROWS):
                wf[r] = wt[r].T
        halo_copies[t].wait_recv()
        crossed = forward(t)
        if t == 3:
            row = 0.5 * moments + place(7, seen + 2.0 * crossed, jnp.zeros((8, W), F32))
            pair_out[1] = jnp.broadcast_to(jnp.sum(row, axis=0, keepdims=True), (8, W))
            pair_copies[1].start()
        if t == 0:
            sn_copy.wait_recv()
            dg[...] = dg[...] + snin[...]
            pout[t] = pout[t] + snin[...] * krylov[t]
        q_copies[t].wait_recv()
        pout[t] = pout[t] + qin[t]
        p_copies[t].start()
        if t == 3:
            all_start(1)
        if t == 1:
            theta = jnp.broadcast_to(all_done(0) * (1.0 / (SLABS * ROWS * W)), (8, W))
            dg[...] = dg[...] - 0.5 * theta
        p_copies[t].wait_recv()
        image = pout[t] + pin[t]
        if t == 1:
            halo_copies[1].wait_send()
            plain = krylov[1]
            one = plain - theta * krylov[0]
            krylov[1] = one
            krylov[2] = image - theta * (plain + one)
            basis_copies[0].start()
            basis_copies[1].start()
        else:
            krylov[t + 1] = image
        if t > 0:
            basis_copies[t + 1].start()

    summed = jnp.broadcast_to(all_done(1), (8, W))
    m = [jnp.broadcast_to(jnp.sum(jnp.where(lane == 8 * sub8 + k, summed, 0.0), axis=1, keepdims=True), (8, W)) for k in range(8)]

    def dot(p, q):
        n = {}
        for i, u in enumerate(p):
            for j, v in enumerate(q):
                n[i + j] = n[i + j] + u * v if i + j in n else u * v
        total = None
        for k, u in n.items():
            total = u * m[k] if total is None else total + u * m[k]
        return total

    one = jnp.ones((8, W), F32)
    res, direction, sol = [one], [one], []
    rr = m[0]
    for it in range(ITERS):
        n = len(direction)
        image = [theta * direction[0]] + [direction[i - 1] + theta * direction[i] for i in range(1, n)] + [direction[-1]]
        alpha = rr / dot(direction, image)
        sol = [(sol[i] + alpha * direction[i]) if i < len(sol) else alpha * direction[i] for i in range(n)]
        res = [(res[i] - alpha * image[i]) if i < len(res) else -alpha * image[i] for i in range(n + 1)]
        if it < ITERS - 1:
            new = dot(res, res)
            beta = new / rr
            direction = [(res[i] + beta * direction[i]) if i < n else res[i] for i in range(n + 1)]
            rr = new
    for i in range(ITERS):
        sol_ref[i] = sol[i]
    sol_ref[ITERS] = jnp.zeros((8, W), F32)
    for i in range(ITERS + 1):
        res_ref[i] = res[i]

    for cp in basis_copies:
        cp.wait()
    sn_copy.wait_send()
    for i in range(2):
        pair_copies[i].wait_send()
        all_copy(i).wait_send()
    for t in range(ITERS):
        if t != 1:
            halo_copies[t].wait_send()
        q_copies[t].wait_send()
        p_copies[t].wait_send()


def body(right_side, diagonal, dense_blocks, tiles, tile_cols, tile_counts):
    vmem = pl.BlockSpec(memory_space=pltpu.VMEM)
    anym = pl.BlockSpec(memory_space=pl.ANY)
    vec = (ROWS, NRHS, W)
    dma = pltpu.SemaphoreType.DMA
    coef = jax.ShapeDtypeStruct((ITERS + 1, NRHS, W), F32)
    basis, sol, res = pl.pallas_call(
        kernel,
        out_shape=(jax.ShapeDtypeStruct((ITERS + 1,) + vec, F32), coef, coef),
        in_specs=[anym] * 6,
        out_specs=(anym, vmem, vmem),
        scratch_shapes=[
            pltpu.SMEM((SLOTS, ROWS), jnp.int32),
            pltpu.SMEM((ROWS,), jnp.int32),
            pltpu.VMEM((ROWS, W), F32),
            pltpu.VMEM((ROWS, SLOTS, W, W), F32),
            pltpu.VMEM((8, W, W), F32),
            pltpu.VMEM((ROWS, 2 * W, SLOTS * W), BF16),
            pltpu.VMEM((ROWS, SLOTS * W, 2 * W), BF16),
            pltpu.VMEM((8, W, 2 * W), BF16),
            pltpu.VMEM((2 * ROWS * NRHS, 512), BF16),
            pltpu.VMEM((64, 8, W), F32),
            pltpu.VMEM((ITERS + 1,) + vec, F32),
            pltpu.VMEM((ITERS,) + vec, F32),
            pltpu.VMEM((ITERS,) + vec, F32),
            pltpu.VMEM((ITERS,) + vec, F32),
            pltpu.VMEM((ITERS,) + vec, F32),
            pltpu.VMEM((ITERS,) + vec, F32),
            pltpu.VMEM(vec, F32),
            pltpu.VMEM(vec, F32),
            pltpu.VMEM(vec, F32),
            pltpu.VMEM((2 * ROWS, 16, W), BF16),
            pltpu.VMEM((512, 2 * W), BF16),
            pltpu.VMEM((4, 8, W), F32),
            pltpu.VMEM((2, 8, W), F32),
            pltpu.VMEM((2, SLABS - 1, 1, W), F32),
            dma((5,)),
            dma((ITERS + 1,)),
            dma((4,)),
            dma((ITERS,)),
            dma((ITERS,)),
            dma((ITERS,)),
            dma((ITERS,)),
            dma((ITERS,)),
            dma((ITERS,)),
            dma,
            dma,
            dma((2,)),
            dma((2,)),
            dma((2,)),
            dma((2,)),
        ],
        compiler_params=pltpu.CompilerParams(collective_id=0, has_side_effects=True, vmem_limit_bytes=60 << 20),
    )(tile_cols.T, tile_counts, right_side, diagonal, dense_blocks, tiles)
    x = jnp.sum(sol[:, None] * basis, axis=0)
    r = jnp.sum(res[:, None] * basis, axis=0)
    return x, r


def solution(mesh):
    return jax.shard_map(
        body,
        mesh=mesh,
        in_specs=(
            P("slab", None, None),
            P("slab", None),
            P(("slab", "sub"), None, None),
            P("slab", "sub", None, None),
            P("slab", "sub"),
            P("slab"),
        ),
        out_specs=(P("slab", None, None), P("slab", None, None)),
        check_vma=False,
    )
```

```python
import functools
import jax
import jax.numpy as jnp
from jax import lax
from jax.experimental import pallas as pl
from jax.experimental.pallas import tpu as pltpu
from jax.sharding import PartitionSpec as P

MESH = pl.DeviceIdType.MESH
F32 = jnp.float32
BF16 = jnp.bfloat16
ITERS = 4
ROWS = 16
SLOTS = 4
NRHS = 8
W = 128
SLABS = 64


def split(x):
    hi = x.astype(BF16)
    return hi, (x - hi.astype(F32)).astype(BF16)


def far(offset):
    return (sum(v != 0 for v in offset), sum(min(v, 4 - v) for v in offset))


CUBE = sorted([(a, b, d) for a in range(4) for b in range(4) for d in range(4) if (a, b, d) != (0, 0, 0)], key=far, reverse=True)
PLANE = [o for o in CUBE if o[0] == 0]
LINE = [o for o in CUBE if o[1] == 0 and o[2] == 0]


def kernel(cols_hbm, counts_hbm, b_hbm, diag_hbm, dense_hbm, tiles_hbm, krylov, sol_ref, res_ref,
           cols, counts, diag_ref, tf, df, wt, wf, dw, gm, sq, halo, qout, qin, pout, pin, dg, snout, snin, vs, bst,
           pair_out, pair_in, all_in, plane_in, line_in, in_sem, tile_sem, peer_ss, peer_rs, halo_ss, halo_rs, q_ss, q_rs, sn_ss, sn_rs, pair_ss, pair_rs, row_ss, row_rs):
    s = lax.axis_index("slab")
    c = lax.axis_index("sub")
    after = ((s + 1) % SLABS, 1 - c)
    before = ((s + SLABS - 1) % SLABS, 1 - c)
    peer = (s, 1 - c)
    first = s * ROWS

    small_copies = [pltpu.make_async_copy(a, b, in_sem.at[i]) for i, (a, b) in enumerate(
        [(cols_hbm, cols), (counts_hbm, counts), (b_hbm, krylov.at[0]), (diag_hbm, diag_ref), (dense_hbm, df)])]
    tile_copies = [pltpu.make_async_copy(tiles_hbm.at[pl.ds(4 * i, 4)], tf.at[pl.ds(4 * i, 4)], tile_sem.at[i]) for i in range(4)]
    for cp in small_copies[:3] + tile_copies + small_copies[3:]:
        cp.start()

    barrier = pltpu.get_barrier_semaphore()
    for dev in (peer, after, before):
        pl.semaphore_signal(barrier, inc=1, device_id=dev, device_id_type=MESH)

    z, xx, yy = s // 16, (s // 4) % 4, s % 4

    def moved(offset):
        a, b, d = offset
        return (((z + a) % 4) * 16 + ((xx + b) % 4) * 4 + (yy + d) % 4, c)

    for offset in CUBE:
        pl.semaphore_signal(barrier, inc=1, device_id=moved(offset), device_id_type=MESH)

    def remote(src, dst, ss, rs, dev):
        return pltpu.make_async_remote_copy(src_ref=src, dst_ref=dst, send_sem=ss, recv_sem=rs, device_id=dev, device_id_type=MESH)

    small_copies[0].wait()
    small_copies[1].wait()
    lane = lax.broadcasted_iota(jnp.int32, (8, W), 1)
    col_lanes = []
    for g in range(4):
        cv = jnp.zeros((8, W), jnp.int32)
        for u in range(16):
            t = g * 16 + u
            cv = jnp.where(lane // 8 == u, cols[t % SLOTS, t // SLOTS] - first, cv)
        col_lanes.append(cv)
    cv = jnp.concatenate(col_lanes, axis=1)
    sub_of = lax.broadcasted_iota(jnp.int32, (8, 512), 0)
    lane_of = lax.broadcasted_iota(jnp.int32, (8, 512), 1)
    cv = jnp.where(lane_of % 8 == sub_of, cv, -1)
    for j in range(0, 2 * ROWS, 2):
        top = jnp.where(cv == j, 1.0, 0.0)
        low = jnp.where(cv == j + 1, 1.0, 0.0)
        gm[8 * j:8 * j + 16, :] = jnp.concatenate([top, low], axis=0).astype(BF16)

    def own_parts(t):
        for j in range(ROWS):
            hi, lo = split(krylov[t, j])
            vs[j] = jnp.concatenate([hi.astype(F32), lo.astype(F32)], axis=0).astype(BF16)

    small_copies[2].wait()
    own_parts(0)

    def back(r):
        y = vs[r]
        out = jnp.dot(jnp.concatenate([y, y], axis=1), wt[r], preferred_element_type=F32)
        out = out[0:8] + out[8:16]
        for h in range(2):
            pair = jnp.concatenate([out[:, 256 * h:256 * h + W], out[:, 256 * h + W:256 * h + 2 * W]], axis=0)
            hi, lo = split(pair)
            at = (r * SLOTS + 2 * h) * 8
            bst[at:at + 16, 0:W] = hi
            bst[at:at + 16, W:2 * W] = lo

    def spread_q(t):
        spread = jnp.dot(gm[...], bst[...], preferred_element_type=F32)
        spread = (spread[:, :W] + spread[:, W:]).reshape(2 * ROWS, NRHS, W)
        qout[t] = spread[ROWS:]
        pout[t] = spread[:ROWS]

    for i in range(4):
        tile_copies[i].wait()
        for r in range(4 * i, 4 * i + 4):
            for k in range(SLOTS):
                live = jnp.where(c * SLOTS + k < counts[r], 1.0, 0.0).astype(F32)
                t = tf[r, k] * live
                hi, lo = split(t)
                wt[r, 0:W, W * k:W * k + W] = hi
                wt[r, W:2 * W, W * k:W * k + W] = lo
                sq[r * SLOTS + k] = jnp.sum((t * t).reshape(16, 8, W), axis=0)
            back(r)
    spread_q(0)
    pl.semaphore_wait(barrier, SLABS + 2)

    halo_copies = [remote(krylov.at[t], halo.at[t], halo_ss.at[t], halo_rs.at[t], before) for t in range(ITERS)]
    q_copies = [remote(qout.at[t], qin.at[t], q_ss.at[t], q_rs.at[t], after) for t in range(ITERS)]
    p_copies = [remote(pout.at[t], pin.at[t], peer_ss.at[t], peer_rs.at[t], peer) for t in range(ITERS)]
    sn_copy = remote(snout, snin, sn_ss, sn_rs, after)
    pair_copies = [remote(pair_out.at[i], pair_in.at[i], pair_ss.at[i], pair_rs.at[i], peer) for i in range(2)]

    def pair_sum(i):
        pair_copies[i].wait_recv()
        return pair_out[i, 0:1] + pair_in[i, 0:1]

    def row_copies(src, into, i, offsets):
        return [remote(src, into.at[pl.ds(n, 1)], row_ss.at[i], row_rs.at[i], moved(o)) for n, o in enumerate(offsets)]

    def row_all(into, i, count):
        return remote(into.at[pl.ds(0, count)], into.at[pl.ds(0, count)], row_ss.at[i], row_rs.at[i], peer)

    def rows_start(k, row):
        pair_out[2 + k, 0:1] = row
        for cp in row_copies(pair_out.at[2 + k, pl.ds(0, 1)], (plane_in, line_in, all_in)[k], k, (PLANE, LINE, CUBE)[k]):
            cp.start()

    def rows_done(k):
        into, count = ((plane_in, len(PLANE)), (line_in, len(LINE)), (all_in, len(CUBE)))[k]
        row_all(into, k, count).wait_recv()
        into[count:count + 1] = pair_out[2 + k, 0:1]
        return jnp.sum(into[0:count + 1], axis=0, keepdims=True)

    halo_copies[0].start()
    q_copies[0].start()

    sigma = jnp.broadcast_to(jnp.sqrt(jnp.sum(jnp.sum(sq[...], axis=2, keepdims=True), axis=1, keepdims=True)), (64, 8, W))
    sigma2 = sigma.reshape(512, W)
    s_hi = sigma2.astype(BF16)
    rest = sigma2 - s_hi.astype(F32)
    s_mid = rest.astype(BF16)
    s_lo = (rest - s_mid.astype(F32)).astype(BF16)
    scol = jnp.dot(gm[...], jnp.concatenate([s_hi, s_mid], axis=1), preferred_element_type=F32)
    scol = scol[:, :W] + scol[:, W:] + jnp.dot(gm[...], s_lo, preferred_element_type=F32)
    scol = scol.reshape(2 * ROWS, NRHS, W)
    snout[...] = scol[ROWS:]
    sn_copy.start()

    small_copies[3].wait()
    small_copies[4].wait()
    dsum = jnp.zeros((8, W), F32)
    dsig = []
    for j in range(8):
        d = df[j]
        sqd = jnp.sum((d * d).reshape(16, 8, W), axis=0)
        dtot = jnp.sum(jnp.sum(sqd, axis=1, keepdims=True), axis=0, keepdims=True)
        ds = jnp.broadcast_to(jnp.sqrt(dtot), (8, W))
        dsig.append(ds)
        dsum = dsum + ds
    half = 0.5 * diag_ref[...]
    diag_sum = jnp.sum(jnp.sum(half, axis=0, keepdims=True), axis=1, keepdims=True)
    pair_out[0] = (2.0 * jnp.sum(sigma, axis=0) + dsum) * W + diag_sum
    pair_copies[0].start()
    for j in range(8):
        d = df[j]
        hi, lo = split(0.5 * (d + d.T))
        dw[j, :, 0:W] = hi
        dw[j, :, W:2 * W] = lo
    dg[...] = jnp.sum(sigma.reshape(ROWS, SLOTS, 8, W), axis=1) + scol[:ROWS] + half[:, None, :]
    for j in range(8):
        dg[8 * c + j] = dg[8 * c + j] + dsig[j]

    sub8 = lax.broadcasted_iota(jnp.int32, (8, W), 0)

    def place(k, x, row):
        return jnp.where(lane == 8 * sub8 + k, jnp.sum(x, axis=1, keepdims=True), row)

    def inner(i, j):
        return jnp.sum(krylov[i] * krylov[j], axis=0)

    def local_part(t):
        loc = [dg[r] * krylov[t, r] for r in range(ROWS)]
        for r in range(ROWS):
            pout[t, r] = pout[t, r] + loc[r]
        seen = loc[0] * krylov[t, 0]
        for r in range(1, ROWS):
            seen = seen + loc[r] * krylov[t, r]
        for j in range(8):
            out = jnp.dot(vs[8 * c + j], dw[j], preferred_element_type=F32)
            out = out[0:8] + out[8:16]
            out = out[:, :W] + out[:, W:]
            pout[t, 8 * c + j] = pout[t, 8 * c + j] + out
            seen = seen + out * krylov[t, 8 * c + j]
        return seen

    def forward(t):
        for j in range(ROWS):
            hi, lo = split(halo[t, j])
            vs[ROWS + j] = jnp.concatenate([hi.astype(F32), lo.astype(F32)], axis=0).astype(BF16)
        seen = jnp.zeros((8, W), F32)
        for r in range(ROWS):
            x = jnp.concatenate([vs[jnp.clip(cols[k, r] - first, 0, 2 * ROWS - 1)] for k in range(SLOTS)], axis=1)
            out = jnp.dot(x, wf[r], preferred_element_type=F32)
            out = out[0:8] + out[8:16]
            out = out[:, :W] + out[:, W:]
            pout[t, r] = pout[t, r] + out
            seen = seen + out * krylov[t, r]
        return seen

    moments = jnp.zeros((8, W), F32)
    theta = None
    for t in range(ITERS):
        if t > 0:
            halo_copies[t].start()
            own_parts(t)
            for r in range(ROWS):
                back(r)
            spread_q(t)
            q_copies[t].start()
        seen = local_part(t)
        if t == 2:
            for i, j in [(0, 0), (0, 1), (1, 1), (1, 2), (2, 2)]:
                moments = place(i + j, inner(i, j), moments)
        if t == 3:
            for i, j in [(2, 3), (3, 3)]:
                moments = place(i + j, inner(i, j), moments)
        if t == 0:
            for r in range(8):
                wf[r] = wt[r].T
            rows_start(0, pair_sum(0))
            for r in range(8, ROWS):
                wf[r] = wt[r].T
        halo_copies[t].wait_recv()
        crossed = forward(t)
        if t == 3:
            row = 0.5 * moments + place(7, seen + 2.0 * crossed, jnp.zeros((8, W), F32))
            pair_out[1] = jnp.broadcast_to(jnp.sum(row, axis=0, keepdims=True), (8, W))
            pair_copies[1].start()
        if t == 0:
            sn_copy.wait_recv()
            dg[...] = dg[...] + snin[...]
            pout[t] = pout[t] + snin[...] * krylov[t]
        q_copies[t].wait_recv()
        pout[t] = pout[t] + qin[t]
        p_copies[t].start()
        if t == 3:
            rows_start(2, pair_sum(1))
        if t == 0:
            rows_start(1, rows_done(0))
        if t == 1:
            theta = jnp.broadcast_to(rows_done(1) * (1.0 / (SLABS * ROWS * W)), (8, W))
            dg[...] = dg[...] - 0.5 * theta
        p_copies[t].wait_recv()
        image = pout[t] + pin[t]
        if t == 1:
            halo_copies[1].wait_send()
            plain = krylov[1]
            one = plain - theta * krylov[0]
            krylov[1] = one
            krylov[2] = image - theta * (plain + one)
        else:
            krylov[t + 1] = image

    summed = jnp.broadcast_to(rows_done(2), (8, W))
    m = [jnp.broadcast_to(jnp.sum(jnp.where(lane == 8 * sub8 + k, summed, 0.0), axis=1, keepdims=True), (8, W)) for k in range(8)]

    def dot(p, q):
        n = {}
        for i, u in enumerate(p):
            for j, v in enumerate(q):
                n[i + j] = n[i + j] + u * v if i + j in n else u * v
        total = None
        for k, u in n.items():
            total = u * m[k] if total is None else total + u * m[k]
        return total

    one = jnp.ones((8, W), F32)
    res, direction, sol = [one], [one], []
    rr = m[0]
    for it in range(ITERS):
        n = len(direction)
        image = [theta * direction[0]] + [direction[i - 1] + theta * direction[i] for i in range(1, n)] + [direction[-1]]
        alpha = rr / dot(direction, image)
        sol = [(sol[i] + alpha * direction[i]) if i < len(sol) else alpha * direction[i] for i in range(n)]
        res = [(res[i] - alpha * image[i]) if i < len(res) else -alpha * image[i] for i in range(n + 1)]
        if it < ITERS - 1:
            new = dot(res, res)
            beta = new / rr
            direction = [(res[i] + beta * direction[i]) if i < n else res[i] for i in range(n + 1)]
            rr = new
    for i in range(ITERS):
        sol_ref[i] = sol[i]
    sol_ref[ITERS] = jnp.zeros((8, W), F32)
    for i in range(ITERS + 1):
        res_ref[i] = res[i]

    sn_copy.wait_send()
    for i in range(2):
        pair_copies[i].wait_send()
    for k, (into, group) in enumerate(((plane_in, PLANE), (line_in, LINE), (all_in, CUBE))):
        row_all(into, k, len(group)).wait_send()
    for t in range(ITERS):
        if t != 1:
            halo_copies[t].wait_send()
        q_copies[t].wait_send()
        p_copies[t].wait_send()


def body(right_side, diagonal, dense_blocks, tiles, tile_cols, tile_counts):
    vmem = pl.BlockSpec(memory_space=pltpu.VMEM)
    anym = pl.BlockSpec(memory_space=pl.ANY)
    vec = (ROWS, NRHS, W)
    dma = pltpu.SemaphoreType.DMA
    coef = jax.ShapeDtypeStruct((ITERS + 1, NRHS, W), F32)
    basis, sol, res = pl.pallas_call(
        kernel,
        out_shape=(jax.ShapeDtypeStruct((ITERS + 1,) + vec, F32), coef, coef),
        in_specs=[anym] * 6,
        out_specs=(vmem, vmem, vmem),
        scratch_shapes=[
            pltpu.SMEM((SLOTS, ROWS), jnp.int32),
            pltpu.SMEM((ROWS,), jnp.int32),
            pltpu.VMEM((ROWS, W), F32),
            pltpu.VMEM((ROWS, SLOTS, W, W), F32),
            pltpu.VMEM((8, W, W), F32),
            pltpu.VMEM((ROWS, 2 * W, SLOTS * W), BF16),
            pltpu.VMEM((ROWS, SLOTS * W, 2 * W), BF16),
            pltpu.VMEM((8, W, 2 * W), BF16),
            pltpu.VMEM((2 * ROWS * NRHS, 512), BF16),
            pltpu.VMEM((64, 8, W), F32),
            pltpu.VMEM((ITERS,) + vec, F32),
            pltpu.VMEM((ITERS,) + vec, F32),
            pltpu.VMEM((ITERS,) + vec, F32),
            pltpu.VMEM((ITERS,) + vec, F32),
            pltpu.VMEM((ITERS,) + vec, F32),
            pltpu.VMEM(vec, F32),
            pltpu.VMEM(vec, F32),
            pltpu.VMEM(vec, F32),
            pltpu.VMEM((2 * ROWS, 16, W), BF16),
            pltpu.VMEM((512, 2 * W), BF16),
            pltpu.VMEM((5, 8, W), F32),
            pltpu.VMEM((2, 8, W), F32),
            pltpu.VMEM((SLABS, W), F32),
            pltpu.VMEM((16, W), F32),
            pltpu.VMEM((8, W), F32),
            dma((5,)),
            dma((4,)),
            dma((ITERS,)),
            dma((ITERS,)),
            dma((ITERS,)),
            dma((ITERS,)),
            dma((ITERS,)),
            dma((ITERS,)),
            dma,
            dma,
            dma((2,)),
            dma((2,)),
            dma((3,)),
            dma((3,)),
        ],
        compiler_params=pltpu.CompilerParams(collective_id=0, has_side_effects=True, vmem_limit_bytes=44 << 20),
    )(*[pltpu.with_memory_space_constraint(a, pltpu.HBM) for a in (tile_cols.T, tile_counts, right_side, diagonal, dense_blocks, tiles)])
    x = jnp.sum(sol[:, None] * basis, axis=0)
    r = jnp.sum(res[:, None] * basis, axis=0)
    return x, r


def solution(mesh):
    return jax.shard_map(
        body,
        mesh=mesh,
        in_specs=(
            P("slab", None, None),
            P("slab", None),
            P(("slab", "sub"), None, None),
            P("slab", "sub", None, None),
            P("slab", "sub"),
            P("slab"),
        ),
        out_specs=(P("slab", None, None), P("slab", None, None)),
        check_vma=False,
    )
```

```python
import functools
import jax
import jax.numpy as jnp
from jax import lax
from jax.experimental import pallas as pl
from jax.experimental.pallas import tpu as pltpu
from jax.sharding import PartitionSpec as P

MESH = pl.DeviceIdType.MESH
F32 = jnp.float32
BF16 = jnp.bfloat16
ITERS = 4
ROWS = 16
SLOTS = 4
NRHS = 8
W = 128
SLABS = 64


def split(x):
    hi = x.astype(BF16)
    return hi, (x - hi.astype(F32)).astype(BF16)


def far(offset):
    return (sum(v != 0 for v in offset), sum(min(v, 4 - v) for v in offset))


CUBE = sorted([(a, b, d) for a in range(4) for b in range(4) for d in range(4) if (a, b, d) != (0, 0, 0)], key=far, reverse=True)
AXES = [[tuple(d if i == a else 0 for i in range(3)) for d in (2, 1, 3)] for a in (2, 1, 0)]
GROUPS = AXES + [CUBE]


def kernel(cols_hbm, counts_hbm, b_hbm, diag_hbm, dense_hbm, tiles_hbm, krylov, sol_ref, res_ref,
           cols, counts, diag_ref, tf, df, wt, wf, dw, gm, sq, halo, qout, qin, pout, pin, dg, snout, snin, vs, bst,
           pair_out, pair_in, all_in, y_in, x_in, z_in, in_sem, tile_sem, peer_ss, peer_rs, halo_ss, halo_rs, q_ss, q_rs, sn_ss, sn_rs, pair_ss, pair_rs, row_ss, row_rs):
    s = lax.axis_index("slab")
    c = lax.axis_index("sub")
    after = ((s + 1) % SLABS, 1 - c)
    before = ((s + SLABS - 1) % SLABS, 1 - c)
    peer = (s, 1 - c)
    first = s * ROWS

    small_copies = [pltpu.make_async_copy(a, b, in_sem.at[i]) for i, (a, b) in enumerate(
        [(cols_hbm, cols), (counts_hbm, counts), (b_hbm, krylov.at[0]), (diag_hbm, diag_ref), (dense_hbm, df)])]
    tile_copies = [pltpu.make_async_copy(tiles_hbm.at[pl.ds(4 * i, 4)], tf.at[pl.ds(4 * i, 4)], tile_sem.at[i]) for i in range(4)]
    for cp in small_copies[:3] + tile_copies + small_copies[3:]:
        cp.start()

    barrier = pltpu.get_barrier_semaphore()
    has_after, has_before = s < SLABS - 1, s > 0

    @pl.when(has_after)
    def _():
        pl.semaphore_signal(barrier, inc=1, device_id=after, device_id_type=MESH)

    @pl.when(has_before)
    def _():
        pl.semaphore_signal(barrier, inc=1, device_id=before, device_id_type=MESH)

    @pl.when(jnp.logical_not(has_before))
    def _():
        qin[...] = jnp.zeros_like(qin)
        snin[...] = jnp.zeros_like(snin)

    @pl.when(jnp.logical_not(has_after))
    def _():
        halo[...] = jnp.zeros_like(halo)

    pl.semaphore_signal(barrier, inc=1, device_id=peer, device_id_type=MESH)

    z, xx, yy = s // 16, (s // 4) % 4, s % 4

    def moved(offset):
        a, b, d = offset
        return (((z + a) % 4) * 16 + ((xx + b) % 4) * 4 + (yy + d) % 4, c)

    for offset in AXES[0] + AXES[1] + AXES[2]:
        pl.semaphore_signal(barrier, inc=1, device_id=moved(offset), device_id_type=MESH)

    def remote(src, dst, ss, rs, dev):
        return pltpu.make_async_remote_copy(src_ref=src, dst_ref=dst, send_sem=ss, recv_sem=rs, device_id=dev, device_id_type=MESH)

    small_copies[0].wait()
    small_copies[1].wait()
    lane = lax.broadcasted_iota(jnp.int32, (8, W), 1)
    col_lanes = []
    for g in range(4):
        cv = jnp.zeros((8, W), jnp.int32)
        for u in range(16):
            t = g * 16 + u
            cv = jnp.where(lane // 8 == u, cols[t % SLOTS, t // SLOTS] - first, cv)
        col_lanes.append(cv)
    cv = jnp.concatenate(col_lanes, axis=1)
    sub_of = lax.broadcasted_iota(jnp.int32, (8, 512), 0)
    lane_of = lax.broadcasted_iota(jnp.int32, (8, 512), 1)
    cv = jnp.where(lane_of % 8 == sub_of, cv, -1)
    for j in range(0, 2 * ROWS, 2):
        top = jnp.where(cv == j, 1.0, 0.0)
        low = jnp.where(cv == j + 1, 1.0, 0.0)
        gm[8 * j:8 * j + 16, :] = jnp.concatenate([top, low], axis=0).astype(BF16)

    def own_parts(t):
        for j in range(ROWS):
            hi, lo = split(krylov[t, j])
            vs[j] = jnp.concatenate([hi.astype(F32), lo.astype(F32)], axis=0).astype(BF16)

    small_copies[2].wait()
    own_parts(0)

    def back(r):
        y = vs[r]
        out = jnp.dot(jnp.concatenate([y, y], axis=1), wt[r], preferred_element_type=F32)
        out = out[0:8] + out[8:16]
        for h in range(2):
            pair = jnp.concatenate([out[:, 256 * h:256 * h + W], out[:, 256 * h + W:256 * h + 2 * W]], axis=0)
            hi, lo = split(pair)
            at = (r * SLOTS + 2 * h) * 8
            bst[at:at + 16, 0:W] = hi
            bst[at:at + 16, W:2 * W] = lo

    def spread_q(t):
        spread = jnp.dot(gm[...], bst[...], preferred_element_type=F32)
        spread = (spread[:, :W] + spread[:, W:]).reshape(2 * ROWS, NRHS, W)
        qout[t] = spread[ROWS:]
        pout[t] = spread[:ROWS]

    for i in range(4):
        tile_copies[i].wait()
        for r in range(4 * i, 4 * i + 4):
            for k in range(SLOTS):
                live = jnp.where(c * SLOTS + k < counts[r], 1.0, 0.0).astype(F32)
                t = tf[r, k] * live
                hi, lo = split(t)
                wt[r, 0:W, W * k:W * k + W] = hi
                wt[r, W:2 * W, W * k:W * k + W] = lo
                sq[r * SLOTS + k] = jnp.sum((t * t).reshape(16, 8, W), axis=0)
            back(r)
    spread_q(0)
    pl.semaphore_wait(barrier, 10 + has_after.astype(jnp.int32) + has_before.astype(jnp.int32))

    def when_call(cond, call):
        @pl.when(cond)
        def _():
            call()


    halo_copies = [remote(krylov.at[t], halo.at[t], halo_ss.at[t], halo_rs.at[t], before) for t in range(ITERS)]
    q_copies = [remote(qout.at[t], qin.at[t], q_ss.at[t], q_rs.at[t], after) for t in range(ITERS)]
    p_copies = [remote(pout.at[t], pin.at[t], peer_ss.at[t], peer_rs.at[t], peer) for t in range(ITERS)]
    sn_copy = remote(snout, snin, sn_ss, sn_rs, after)
    pair_copies = [remote(pair_out.at[i], pair_in.at[i], pair_ss.at[i], pair_rs.at[i], peer) for i in range(2)]

    lands = (y_in, x_in, z_in, all_in)

    def pair_sum(i):
        pair_copies[i].wait_recv()
        return pair_out[i, 0:1] + pair_in[i, 0:1]

    def row_copies(src, into, i, offsets):
        return [remote(src, into.at[pl.ds(n, 1)], row_ss.at[i], row_rs.at[i], moved(o)) for n, o in enumerate(offsets)]

    def row_all(into, i, count):
        return remote(into.at[pl.ds(0, count)], into.at[pl.ds(0, count)], row_ss.at[i], row_rs.at[i], peer)

    def rows_start(k, row):
        pair_out[2 + k, 0:1] = row
        for cp in row_copies(pair_out.at[2 + k, pl.ds(0, 1)], lands[k], k, GROUPS[k]):
            cp.start()

    def rows_done(k):
        into, count = lands[k], len(GROUPS[k])
        row_all(into, k, count).wait_recv()
        into[count:count + 1] = pair_out[2 + k, 0:1]
        return jnp.sum(into[0:count + 1], axis=0, keepdims=True)

    when_call(has_before, halo_copies[0].start)
    when_call(has_after, q_copies[0].start)

    sigma = jnp.broadcast_to(jnp.sqrt(jnp.sum(jnp.sum(sq[...], axis=2, keepdims=True), axis=1, keepdims=True)), (64, 8, W))
    sigma2 = sigma.reshape(512, W)
    s_hi = sigma2.astype(BF16)
    rest = sigma2 - s_hi.astype(F32)
    s_mid = rest.astype(BF16)
    s_lo = (rest - s_mid.astype(F32)).astype(BF16)
    scol = jnp.dot(gm[...], jnp.concatenate([s_hi, s_mid], axis=1), preferred_element_type=F32)
    scol = scol[:, :W] + scol[:, W:] + jnp.dot(gm[...], s_lo, preferred_element_type=F32)
    scol = scol.reshape(2 * ROWS, NRHS, W)
    snout[...] = scol[ROWS:]
    when_call(has_after, sn_copy.start)

    small_copies[3].wait()
    small_copies[4].wait()
    dsum = jnp.zeros((8, W), F32)
    dsig = []
    for j in range(8):
        d = df[j]
        sqd = jnp.sum((d * d).reshape(16, 8, W), axis=0)
        dtot = jnp.sum(jnp.sum(sqd, axis=1, keepdims=True), axis=0, keepdims=True)
        ds = jnp.broadcast_to(jnp.sqrt(dtot), (8, W))
        dsig.append(ds)
        dsum = dsum + ds
    half = 0.5 * diag_ref[...]
    diag_sum = jnp.sum(jnp.sum(half, axis=0, keepdims=True), axis=1, keepdims=True)
    pair_out[0] = (2.0 * jnp.sum(sigma, axis=0) + dsum) * W + diag_sum
    pair_copies[0].start()
    for j in range(8):
        d = df[j]
        hi, lo = split(0.5 * (d + d.T))
        dw[j, :, 0:W] = hi
        dw[j, :, W:2 * W] = lo
    dg[...] = jnp.sum(sigma.reshape(ROWS, SLOTS, 8, W), axis=1) + scol[:ROWS] + half[:, None, :]
    for j in range(8):
        dg[8 * c + j] = dg[8 * c + j] + dsig[j]

    sub8 = lax.broadcasted_iota(jnp.int32, (8, W), 0)

    def place(k, x, row):
        return jnp.where(lane == 8 * sub8 + k, jnp.sum(x, axis=1, keepdims=True), row)

    def inner(i, j):
        return jnp.sum(krylov[i] * krylov[j], axis=0)

    def local_part(t):
        loc = [dg[r] * krylov[t, r] for r in range(ROWS)]
        for r in range(ROWS):
            pout[t, r] = pout[t, r] + loc[r]
        seen = loc[0] * krylov[t, 0]
        for r in range(1, ROWS):
            seen = seen + loc[r] * krylov[t, r]
        for j in range(8):
            out = jnp.dot(vs[8 * c + j], dw[j], preferred_element_type=F32)
            out = out[0:8] + out[8:16]
            out = out[:, :W] + out[:, W:]
            pout[t, 8 * c + j] = pout[t, 8 * c + j] + out
            seen = seen + out * krylov[t, 8 * c + j]
        return seen

    def forward(t):
        for j in range(ROWS):
            hi, lo = split(halo[t, j])
            vs[ROWS + j] = jnp.concatenate([hi.astype(F32), lo.astype(F32)], axis=0).astype(BF16)
        seen = jnp.zeros((8, W), F32)
        for r in range(ROWS):
            x = jnp.concatenate([vs[jnp.clip(cols[k, r] - first, 0, 2 * ROWS - 1)] for k in range(SLOTS)], axis=1)
            out = jnp.dot(x, wf[r], preferred_element_type=F32)
            out = out[0:8] + out[8:16]
            out = out[:, :W] + out[:, W:]
            pout[t, r] = pout[t, r] + out
            seen = seen + out * krylov[t, r]
        return seen

    moments = jnp.zeros((8, W), F32)
    theta = None
    for t in range(ITERS):
        if t > 0:
            when_call(has_before, halo_copies[t].start)
            own_parts(t)
            for r in range(ROWS):
                back(r)
            spread_q(t)
            when_call(has_after, q_copies[t].start)
        seen = local_part(t)
        if t == 2:
            for i, j in [(0, 0), (0, 1), (1, 1), (1, 2), (2, 2)]:
                moments = place(i + j, inner(i, j), moments)
        if t == 3:
            for i, j in [(2, 3), (3, 3)]:
                moments = place(i + j, inner(i, j), moments)
        if t == 0:
            for r in range(8):
                wf[r] = wt[r].T
            rows_start(0, pair_sum(0))
            for r in range(8, ROWS):
                wf[r] = wt[r].T
        if t == 1:
            rows_start(2, rows_done(1))
        when_call(has_after, halo_copies[t].wait_recv)
        crossed = forward(t)
        if t == 3:
            row = 0.5 * moments + place(7, seen + 2.0 * crossed, jnp.zeros((8, W), F32))
            pair_out[1] = jnp.broadcast_to(jnp.sum(row, axis=0, keepdims=True), (8, W))
            pair_copies[1].start()
        if t == 0:
            when_call(has_before, sn_copy.wait_recv)
            dg[...] = dg[...] + snin[...]
            pout[t] = pout[t] + snin[...] * krylov[t]
        when_call(has_before, q_copies[t].wait_recv)
        pout[t] = pout[t] + qin[t]
        p_copies[t].start()
        if t == 3:
            rows_start(3, pair_sum(1))
        if t == 0:
            rows_start(1, rows_done(0))
        if t == 1:
            theta = jnp.broadcast_to(rows_done(2) * (1.0 / (SLABS * ROWS * W)), (8, W))
            dg[...] = dg[...] - 0.5 * theta
        p_copies[t].wait_recv()
        image = pout[t] + pin[t]
        if t == 1:
            when_call(has_before, halo_copies[1].wait_send)
            plain = krylov[1]
            one = plain - theta * krylov[0]
            krylov[1] = one
            krylov[2] = image - theta * (plain + one)
        else:
            krylov[t + 1] = image

    summed = jnp.broadcast_to(rows_done(3), (8, W))
    m = [jnp.broadcast_to(jnp.sum(jnp.where(lane == 8 * sub8 + k, summed, 0.0), axis=1, keepdims=True), (8, W)) for k in range(8)]

    def dot(p, q):
        n = {}
        for i, u in enumerate(p):
            for j, v in enumerate(q):
                n[i + j] = n[i + j] + u * v if i + j in n else u * v
        total = None
        for k, u in n.items():
            total = u * m[k] if total is None else total + u * m[k]
        return total

    one = jnp.ones((8, W), F32)
    res, direction, sol = [one], [one], []
    rr = m[0]
    for it in range(ITERS):
        n = len(direction)
        image = [theta * direction[0]] + [direction[i - 1] + theta * direction[i] for i in range(1, n)] + [direction[-1]]
        alpha = rr / dot(direction, image)
        sol = [(sol[i] + alpha * direction[i]) if i < len(sol) else alpha * direction[i] for i in range(n)]
        res = [(res[i] - alpha * image[i]) if i < len(res) else -alpha * image[i] for i in range(n + 1)]
        if it < ITERS - 1:
            new = dot(res, res)
            beta = new / rr
            direction = [(res[i] + beta * direction[i]) if i < n else res[i] for i in range(n + 1)]
            rr = new
    for i in range(ITERS):
        sol_ref[i] = sol[i]
    sol_ref[ITERS] = jnp.zeros((8, W), F32)
    for i in range(ITERS + 1):
        res_ref[i] = res[i]

    when_call(has_after, sn_copy.wait_send)
    for i in range(2):
        pair_copies[i].wait_send()
    for k, (into, group) in enumerate(zip(lands, GROUPS)):
        row_all(into, k, len(group)).wait_send()
    for t in range(ITERS):
        if t != 1:
            when_call(has_before, halo_copies[t].wait_send)
        when_call(has_after, q_copies[t].wait_send)
        p_copies[t].wait_send()


def body(right_side, diagonal, dense_blocks, tiles, tile_cols, tile_counts):
    vmem = pl.BlockSpec(memory_space=pltpu.VMEM)
    anym = pl.BlockSpec(memory_space=pl.ANY)
    vec = (ROWS, NRHS, W)
    dma = pltpu.SemaphoreType.DMA
    coef = jax.ShapeDtypeStruct((ITERS + 1, NRHS, W), F32)
    basis, sol, res = pl.pallas_call(
        kernel,
        out_shape=(jax.ShapeDtypeStruct((ITERS + 1,) + vec, F32), coef, coef),
        in_specs=[anym] * 6,
        out_specs=(vmem, vmem, vmem),
        scratch_shapes=[
            pltpu.SMEM((SLOTS, ROWS), jnp.int32),
            pltpu.SMEM((ROWS,), jnp.int32),
            pltpu.VMEM((ROWS, W), F32),
            pltpu.VMEM((ROWS, SLOTS, W, W), F32),
            pltpu.VMEM((8, W, W), F32),
            pltpu.VMEM((ROWS, 2 * W, SLOTS * W), BF16),
            pltpu.VMEM((ROWS, SLOTS * W, 2 * W), BF16),
            pltpu.VMEM((8, W, 2 * W), BF16),
            pltpu.VMEM((2 * ROWS * NRHS, 512), BF16),
            pltpu.VMEM((64, 8, W), F32),
            pltpu.VMEM((ITERS,) + vec, F32),
            pltpu.VMEM((ITERS,) + vec, F32),
            pltpu.VMEM((ITERS,) + vec, F32),
            pltpu.VMEM((ITERS,) + vec, F32),
            pltpu.VMEM((ITERS,) + vec, F32),
            pltpu.VMEM(vec, F32),
            pltpu.VMEM(vec, F32),
            pltpu.VMEM(vec, F32),
            pltpu.VMEM((2 * ROWS, 16, W), BF16),
            pltpu.VMEM((512, 2 * W), BF16),
            pltpu.VMEM((6, 8, W), F32),
            pltpu.VMEM((2, 8, W), F32),
            pltpu.VMEM((SLABS, W), F32),
            pltpu.VMEM((8, W), F32),
            pltpu.VMEM((8, W), F32),
            pltpu.VMEM((8, W), F32),
            dma((5,)),
            dma((4,)),
            dma((ITERS,)),
            dma((ITERS,)),
            dma((ITERS,)),
            dma((ITERS,)),
            dma((ITERS,)),
            dma((ITERS,)),
            dma,
            dma,
            dma((2,)),
            dma((2,)),
            dma((4,)),
            dma((4,)),
        ],
        compiler_params=pltpu.CompilerParams(collective_id=0, has_side_effects=True, vmem_limit_bytes=44 << 20),
    )(*[pltpu.with_memory_space_constraint(a, pltpu.HBM) for a in (tile_cols.T, tile_counts, right_side, diagonal, dense_blocks, tiles)])
    x = jnp.sum(sol[:, None] * basis, axis=0)
    r = jnp.sum(res[:, None] * basis, axis=0)
    return x, r


def solution(mesh):
    return jax.shard_map(
        body,
        mesh=mesh,
        in_specs=(
            P("slab", None, None),
            P("slab", None),
            P(("slab", "sub"), None, None),
            P("slab", "sub", None, None),
            P("slab", "sub"),
            P("slab"),
        ),
        out_specs=(P("slab", None, None), P("slab", None, None)),
        check_vma=False,
    )
```

```python
import functools
import jax
import jax.numpy as jnp
from jax import lax
from jax.experimental import pallas as pl
from jax.experimental.pallas import tpu as pltpu
from jax.sharding import PartitionSpec as P

MESH = pl.DeviceIdType.MESH
F32 = jnp.float32
BF16 = jnp.bfloat16
ITERS = 4
ROWS = 16
SLOTS = 4
NRHS = 8
W = 128
SLABS = 64


def split(x):
    hi = x.astype(BF16)
    return hi, (x - hi.astype(F32)).astype(BF16)


def far(offset):
    return (sum(v != 0 for v in offset), sum(min(v, 4 - v) for v in offset))


CUBE = sorted([(a, b, d) for a in range(4) for b in range(4) for d in range(4) if (a, b, d) != (0, 0, 0)], key=far, reverse=True)
AXES = [[tuple(d if i == a else 0 for i in range(3)) for d in (2, 1, 3)] for a in (2, 1, 0)]
GROUPS = AXES + [CUBE]


def kernel(cols_hbm, counts_hbm, b_hbm, diag_hbm, dense_hbm, tiles_hbm, krylov, sol_ref, res_ref,
           cols, counts, diag_ref, tf, df, wt, wf, dw, gm, sq, halo, qout, qin, pout, pin, dg, snout, snin, vs, bst,
           pair_out, pair_in, all_in, y_in, x_in, z_in, in_sem, tile_sem, peer_ss, peer_rs, halo_ss, halo_rs, q_ss, q_rs, sn_ss, sn_rs, pair_ss, pair_rs, row_ss, row_rs):
    s = lax.axis_index("slab")
    c = lax.axis_index("sub")
    after = ((s + 1) % SLABS, 1 - c)
    before = ((s + SLABS - 1) % SLABS, 1 - c)
    peer = (s, 1 - c)
    first = s * ROWS

    small_copies = [pltpu.make_async_copy(a, b, in_sem.at[i]) for i, (a, b) in enumerate(
        [(cols_hbm, cols), (counts_hbm, counts), (b_hbm, krylov.at[0]), (diag_hbm, diag_ref), (dense_hbm, df)])]
    tile_copies = [pltpu.make_async_copy(tiles_hbm.at[pl.ds(4 * i, 4)], tf.at[pl.ds(4 * i, 4)], tile_sem.at[i]) for i in range(4)]
    for cp in small_copies[:3] + tile_copies + small_copies[3:]:
        cp.start()

    barrier = pltpu.get_barrier_semaphore()
    has_after, has_before = s < SLABS - 1, s > 0

    @pl.when(has_after)
    def _():
        pl.semaphore_signal(barrier, inc=1, device_id=after, device_id_type=MESH)

    @pl.when(has_before)
    def _():
        pl.semaphore_signal(barrier, inc=1, device_id=before, device_id_type=MESH)

    @pl.when(jnp.logical_not(has_before))
    def _():
        qin[...] = jnp.zeros_like(qin)
        snin[...] = jnp.zeros_like(snin)

    @pl.when(jnp.logical_not(has_after))
    def _():
        halo[...] = jnp.zeros_like(halo)

    pl.semaphore_signal(barrier, inc=1, device_id=peer, device_id_type=MESH)

    z, xx, yy = s // 16, (s // 4) % 4, s % 4

    def moved(offset):
        a, b, d = offset
        return (((z + a) % 4) * 16 + ((xx + b) % 4) * 4 + (yy + d) % 4, c)

    for offset in AXES[0] + AXES[1] + AXES[2]:
        pl.semaphore_signal(barrier, inc=1, device_id=moved(offset), device_id_type=MESH)

    def remote(src, dst, ss, rs, dev):
        return pltpu.make_async_remote_copy(src_ref=src, dst_ref=dst, send_sem=ss, recv_sem=rs, device_id=dev, device_id_type=MESH)

    small_copies[0].wait()
    small_copies[1].wait()
    lane = lax.broadcasted_iota(jnp.int32, (8, W), 1)
    col_lanes = []
    for g in range(4):
        cv = jnp.zeros((8, W), jnp.int32)
        for u in range(16):
            t = g * 16 + u
            cv = jnp.where(lane // 8 == u, cols[t % SLOTS, t // SLOTS] - first, cv)
        col_lanes.append(cv)
    cv = jnp.concatenate(col_lanes, axis=1)
    sub_of = lax.broadcasted_iota(jnp.int32, (8, 512), 0)
    lane_of = lax.broadcasted_iota(jnp.int32, (8, 512), 1)
    cv = jnp.where(lane_of % 8 == sub_of, cv, -1)
    for j in range(0, 2 * ROWS, 2):
        top = jnp.where(cv == j, 1.0, 0.0)
        low = jnp.where(cv == j + 1, 1.0, 0.0)
        gm[8 * j:8 * j + 16, :] = jnp.concatenate([top, low], axis=0).astype(BF16)

    def own_parts(t):
        for j in range(ROWS):
            hi, lo = split(krylov[t, j])
            vs[j] = jnp.concatenate([hi.astype(F32), lo.astype(F32)], axis=0).astype(BF16)

    small_copies[2].wait()
    own_parts(0)

    def back(r):
        y = vs[r]
        out = jnp.dot(jnp.concatenate([y, y], axis=1), wt[r], preferred_element_type=F32)
        out = out[0:8] + out[8:16]
        for h in range(2):
            pair = jnp.concatenate([out[:, 256 * h:256 * h + W], out[:, 256 * h + W:256 * h + 2 * W]], axis=0)
            hi, lo = split(pair)
            at = (r * SLOTS + 2 * h) * 8
            bst[at:at + 16, 0:W] = hi
            bst[at:at + 16, W:2 * W] = lo

    def spread_high(t):
        spread = jnp.dot(gm[192:256, 256:512], bst[256:512, :], preferred_element_type=F32)
        qout[t, 8:ROWS] = (spread[:, :W] + spread[:, W:]).reshape(8, NRHS, W)

    def spread_low(t):
        spread = jnp.dot(gm[0:192, :], bst[...], preferred_element_type=F32)
        spread = (spread[:, :W] + spread[:, W:]).reshape(24, NRHS, W)
        qout[t, 0:8] = spread[ROWS:]
        pout[t] = spread[:ROWS]

    for i in range(4):
        tile_copies[i].wait()
        for r in range(4 * i, 4 * i + 4):
            for k in range(SLOTS):
                live = jnp.where(c * SLOTS + k < counts[r], 1.0, 0.0).astype(F32)
                t = tf[r, k] * live
                hi, lo = split(t)
                wt[r, 0:W, W * k:W * k + W] = hi
                wt[r, W:2 * W, W * k:W * k + W] = lo
                sq[r * SLOTS + k] = jnp.sum((t * t).reshape(16, 8, W), axis=0)
            back(r)
    spread_high(0)
    spread_low(0)
    pl.semaphore_wait(barrier, 10 + has_after.astype(jnp.int32) + has_before.astype(jnp.int32))

    def when_call(cond, call):
        @pl.when(cond)
        def _():
            call()


    def halves(src, into, ss, rs, dev):
        return [[remote(src.at[t, pl.ds(8 * h, 8)], into.at[t, pl.ds(8 * h, 8)], ss.at[t, h], rs.at[t, h], dev) for h in range(2)] for t in range(ITERS)]

    halo_copies = halves(krylov, halo, halo_ss, halo_rs, before)
    q_copies = halves(qout, qin, q_ss, q_rs, after)
    p_copies = halves(pout, pin, peer_ss, peer_rs, peer)
    sn_copy = remote(snout, snin, sn_ss, sn_rs, after)
    pair_copies = [remote(pair_out.at[i], pair_in.at[i], pair_ss.at[i], pair_rs.at[i], peer) for i in range(2)]

    lands = (y_in, x_in, z_in, all_in)

    def pair_sum(i):
        pair_copies[i].wait_recv()
        return pair_out[i, 0:1] + pair_in[i, 0:1]

    def row_copies(src, into, i, offsets):
        return [remote(src, into.at[pl.ds(n, 1)], row_ss.at[i], row_rs.at[i], moved(o)) for n, o in enumerate(offsets)]

    def row_all(into, i, count):
        return remote(into.at[pl.ds(0, count)], into.at[pl.ds(0, count)], row_ss.at[i], row_rs.at[i], peer)

    def rows_start(k, row):
        pair_out[2 + k, 0:1] = row
        for cp in row_copies(pair_out.at[2 + k, pl.ds(0, 1)], lands[k], k, GROUPS[k]):
            cp.start()

    def rows_done(k):
        into, count = lands[k], len(GROUPS[k])
        row_all(into, k, count).wait_recv()
        into[count:count + 1] = pair_out[2 + k, 0:1]
        return jnp.sum(into[0:count + 1], axis=0, keepdims=True)

    for h in range(2):
        when_call(has_before, halo_copies[0][h].start)
    for h in (1, 0):
        when_call(has_after, q_copies[0][h].start)

    sigma = jnp.broadcast_to(jnp.sqrt(jnp.sum(jnp.sum(sq[...], axis=2, keepdims=True), axis=1, keepdims=True)), (64, 8, W))
    sigma2 = sigma.reshape(512, W)
    s_hi = sigma2.astype(BF16)
    rest = sigma2 - s_hi.astype(F32)
    s_mid = rest.astype(BF16)
    s_lo = (rest - s_mid.astype(F32)).astype(BF16)
    scol = jnp.dot(gm[...], jnp.concatenate([s_hi, s_mid], axis=1), preferred_element_type=F32)
    scol = scol[:, :W] + scol[:, W:] + jnp.dot(gm[...], s_lo, preferred_element_type=F32)
    scol = scol.reshape(2 * ROWS, NRHS, W)
    snout[...] = scol[ROWS:]
    when_call(has_after, sn_copy.start)

    small_copies[3].wait()
    small_copies[4].wait()
    dsum = jnp.zeros((8, W), F32)
    dsig = []
    for j in range(8):
        d = df[j]
        sqd = jnp.sum((d * d).reshape(16, 8, W), axis=0)
        dtot = jnp.sum(jnp.sum(sqd, axis=1, keepdims=True), axis=0, keepdims=True)
        ds = jnp.broadcast_to(jnp.sqrt(dtot), (8, W))
        dsig.append(ds)
        dsum = dsum + ds
    half = 0.5 * diag_ref[...]
    diag_sum = jnp.sum(jnp.sum(half, axis=0, keepdims=True), axis=1, keepdims=True)
    pair_out[0] = (2.0 * jnp.sum(sigma, axis=0) + dsum) * W + diag_sum
    pair_copies[0].start()
    for j in range(8):
        d = df[j]
        hi, lo = split(0.5 * (d + d.T))
        dw[j, :, 0:W] = hi
        dw[j, :, W:2 * W] = lo
    dg[...] = jnp.sum(sigma.reshape(ROWS, SLOTS, 8, W), axis=1) + scol[:ROWS] + half[:, None, :]
    for j in range(8):
        dg[8 * c + j] = dg[8 * c + j] + dsig[j]

    sub8 = lax.broadcasted_iota(jnp.int32, (8, W), 0)

    def place(k, x, row):
        return jnp.where(lane == 8 * sub8 + k, jnp.sum(x, axis=1, keepdims=True), row)

    def inner(i, j):
        return jnp.sum(krylov[i] * krylov[j], axis=0)

    def local_part(t):
        loc = [dg[r] * krylov[t, r] for r in range(ROWS)]
        for r in range(ROWS):
            pout[t, r] = pout[t, r] + loc[r]
        seen = loc[0] * krylov[t, 0]
        for r in range(1, ROWS):
            seen = seen + loc[r] * krylov[t, r]
        for j in range(8):
            out = jnp.dot(vs[8 * c + j], dw[j], preferred_element_type=F32)
            out = out[0:8] + out[8:16]
            out = out[:, :W] + out[:, W:]
            pout[t, 8 * c + j] = pout[t, 8 * c + j] + out
            seen = seen + out * krylov[t, 8 * c + j]
        return seen

    def forward(t, h):
        for j in range(8 * h, 8 * h + 8):
            hi, lo = split(halo[t, j])
            vs[ROWS + j] = jnp.concatenate([hi.astype(F32), lo.astype(F32)], axis=0).astype(BF16)
        seen = jnp.zeros((8, W), F32)
        for r in range(8 * h, 8 * h + 8):
            x = jnp.concatenate([vs[jnp.clip(cols[k, r] - first, 0, ROWS + 8 * h + 7)] for k in range(SLOTS)], axis=1)
            out = jnp.dot(x, wf[r], preferred_element_type=F32)
            out = out[0:8] + out[8:16]
            out = out[:, :W] + out[:, W:]
            pout[t, r] = pout[t, r] + out
            seen = seen + out * krylov[t, r]
        return seen

    moments = jnp.zeros((8, W), F32)
    theta = None
    for t in range(ITERS):
        if t > 0:
            for h in range(2):
                when_call(has_before, halo_copies[t][h].start)
            own_parts(t)
            for r in range(8, ROWS):
                back(r)
            spread_high(t)
            when_call(has_after, q_copies[t][1].start)
            for r in range(8):
                back(r)
            spread_low(t)
            when_call(has_after, q_copies[t][0].start)
        seen = local_part(t)
        if t == 2:
            for i, j in [(0, 0), (0, 1), (1, 1), (1, 2), (2, 2)]:
                moments = place(i + j, inner(i, j), moments)
        if t == 3:
            for i, j in [(2, 3), (3, 3)]:
                moments = place(i + j, inner(i, j), moments)
        if t == 0:
            for r in range(8):
                wf[r] = wt[r].T
            rows_start(0, pair_sum(0))
            for r in range(8, ROWS):
                wf[r] = wt[r].T
        if t == 1:
            rows_start(2, rows_done(1))
        crossed = seen * 0.5
        for h in range(2):
            when_call(has_after, halo_copies[t][h].wait_recv)
            crossed = crossed + forward(t, h)
        if t == 3:
            row = 0.5 * moments + place(7, 2.0 * crossed, jnp.zeros((8, W), F32))
            pair_out[1] = jnp.broadcast_to(jnp.sum(row, axis=0, keepdims=True), (8, W))
            pair_copies[1].start()
            rows_start(3, pair_sum(1))
        if t == 0:
            when_call(has_before, sn_copy.wait_recv)
            dg[...] = dg[...] + snin[...]
            pout[t] = pout[t] + snin[...] * krylov[t]
        for h in (1, 0):
            when_call(has_before, q_copies[t][h].wait_recv)
            pout[t, 8 * h:8 * h + 8] = pout[t, 8 * h:8 * h + 8] + qin[t, 8 * h:8 * h + 8]
            p_copies[t][h].start()
        if t == 0:
            rows_start(1, rows_done(0))
        if t == 1:
            theta = jnp.broadcast_to(rows_done(2) * (1.0 / (SLABS * ROWS * W)), (8, W))
            dg[...] = dg[...] - 0.5 * theta
        p_copies[t][1].wait_recv()
        p_copies[t][0].wait_recv()
        image = pout[t] + pin[t]
        if t == 1:
            for h in range(2):
                when_call(has_before, halo_copies[1][h].wait_send)
            plain = krylov[1]
            one = plain - theta * krylov[0]
            krylov[1] = one
            krylov[2] = image - theta * (plain + one)
        else:
            krylov[t + 1] = image

    summed = jnp.broadcast_to(rows_done(3), (8, W))
    m = [jnp.broadcast_to(jnp.sum(jnp.where(lane == 8 * sub8 + k, summed, 0.0), axis=1, keepdims=True), (8, W)) for k in range(8)]

    def dot(p, q):
        n = {}
        for i, u in enumerate(p):
            for j, v in enumerate(q):
                n[i + j] = n[i + j] + u * v if i + j in n else u * v
        total = None
        for k, u in n.items():
            total = u * m[k] if total is None else total + u * m[k]
        return total

    one = jnp.ones((8, W), F32)
    res, direction, sol = [one], [one], []
    rr = m[0]
    for it in range(ITERS):
        n = len(direction)
        image = [theta * direction[0]] + [direction[i - 1] + theta * direction[i] for i in range(1, n)] + [direction[-1]]
        alpha = rr / dot(direction, image)
        sol = [(sol[i] + alpha * direction[i]) if i < len(sol) else alpha * direction[i] for i in range(n)]
        res = [(res[i] - alpha * image[i]) if i < len(res) else -alpha * image[i] for i in range(n + 1)]
        if it < ITERS - 1:
            new = dot(res, res)
            beta = new / rr
            direction = [(res[i] + beta * direction[i]) if i < n else res[i] for i in range(n + 1)]
            rr = new
    for i in range(ITERS):
        sol_ref[i] = sol[i]
    sol_ref[ITERS] = jnp.zeros((8, W), F32)
    for i in range(ITERS + 1):
        res_ref[i] = res[i]

    when_call(has_after, sn_copy.wait_send)
    for i in range(2):
        pair_copies[i].wait_send()
    for k, (into, group) in enumerate(zip(lands, GROUPS)):
        row_all(into, k, len(group)).wait_send()
    for t in range(ITERS):
        for h in range(2):
            if t != 1:
                when_call(has_before, halo_copies[t][h].wait_send)
            when_call(has_after, q_copies[t][h].wait_send)
            p_copies[t][h].wait_send()


def body(right_side, diagonal, dense_blocks, tiles, tile_cols, tile_counts):
    vmem = pl.BlockSpec(memory_space=pltpu.VMEM)
    anym = pl.BlockSpec(memory_space=pl.ANY)
    vec = (ROWS, NRHS, W)
    dma = pltpu.SemaphoreType.DMA
    coef = jax.ShapeDtypeStruct((ITERS + 1, NRHS, W), F32)
    basis, sol, res = pl.pallas_call(
        kernel,
        out_shape=(jax.ShapeDtypeStruct((ITERS + 1,) + vec, F32), coef, coef),
        in_specs=[anym] * 6,
        out_specs=(vmem, vmem, vmem),
        scratch_shapes=[
            pltpu.SMEM((SLOTS, ROWS), jnp.int32),
            pltpu.SMEM((ROWS,), jnp.int32),
            pltpu.VMEM((ROWS, W), F32),
            pltpu.VMEM((ROWS, SLOTS, W, W), F32),
            pltpu.VMEM((8, W, W), F32),
            pltpu.VMEM((ROWS, 2 * W, SLOTS * W), BF16),
            pltpu.VMEM((ROWS, SLOTS * W, 2 * W), BF16),
            pltpu.VMEM((8, W, 2 * W), BF16),
            pltpu.VMEM((2 * ROWS * NRHS, 512), BF16),
            pltpu.VMEM((64, 8, W), F32),
            pltpu.VMEM((ITERS,) + vec, F32),
            pltpu.VMEM((ITERS,) + vec, F32),
            pltpu.VMEM((ITERS,) + vec, F32),
            pltpu.VMEM((ITERS,) + vec, F32),
            pltpu.VMEM((ITERS,) + vec, F32),
            pltpu.VMEM(vec, F32),
            pltpu.VMEM(vec, F32),
            pltpu.VMEM(vec, F32),
            pltpu.VMEM((2 * ROWS, 16, W), BF16),
            pltpu.VMEM((512, 2 * W), BF16),
            pltpu.VMEM((6, 8, W), F32),
            pltpu.VMEM((2, 8, W), F32),
            pltpu.VMEM((SLABS, W), F32),
            pltpu.VMEM((8, W), F32),
            pltpu.VMEM((8, W), F32),
            pltpu.VMEM((8, W), F32),
            dma((5,)),
            dma((4,)),
            dma((ITERS, 2)),
            dma((ITERS, 2)),
            dma((ITERS, 2)),
            dma((ITERS, 2)),
            dma((ITERS, 2)),
            dma((ITERS, 2)),
            dma,
            dma,
            dma((2,)),
            dma((2,)),
            dma((4,)),
            dma((4,)),
        ],
        compiler_params=pltpu.CompilerParams(collective_id=0, has_side_effects=True, vmem_limit_bytes=44 << 20),
    )(*[pltpu.with_memory_space_constraint(a, pltpu.HBM) for a in (tile_cols.T, tile_counts, right_side, diagonal, dense_blocks, tiles)])
    x = jnp.sum(sol[:, None] * basis, axis=0)
    r = jnp.sum(res[:, None] * basis, axis=0)
    return x, r


def solution(mesh):
    return jax.shard_map(
        body,
        mesh=mesh,
        in_specs=(
            P("slab", None, None),
            P("slab", None),
            P(("slab", "sub"), None, None),
            P("slab", "sub", None, None),
            P("slab", "sub"),
            P("slab"),
        ),
        out_specs=(P("slab", None, None), P("slab", None, None)),
        check_vma=False,
    )
```
